32 devices in a mesh: row: 4 (over y, x), ch: 8 (over z, core).
Axes of the slice: x: 2, y: 2, z: 4, core: 2. Of those that a mesh axis runs over, the one named last changes fastest.
Arguments:
- features: bfloat16 [4, 256, 4096], P('row', None, 'ch'), may hold values from -6 to 6
- w_in: bfloat16 [4096, 4096], P(None, 'ch'), may hold values from -0.125 to 0.125
- w_group: bfloat16 [3, 3, 64, 4096], P(None, None, None, 'ch'), may hold values from -0.25 to 0.25
- w_out: bfloat16 [4096, 4096], P(None, 'ch'), may hold values from -0.125 to 0.125
- cotangent: bfloat16 [4, 256, 4096], P('row', None, 'ch'), may hold values from -6 to 6
Outputs:
- block_out: bfloat16 [4, 256, 4096], P('row', None, 'ch')
- grad_input: bfloat16 [4, 256, 4096], P('row', None, 'ch')
- grad_w_in: bfloat16 [4096, 4096], P(None, 'ch')
- grad_w_group: bfloat16 [3, 3, 64, 4096], P(None, None, None, 'ch')
- grad_w_out: bfloat16 [4096, 4096], P(None, 'ch')
The draws below stay inside these ranges and needn't reach their ends.
All inputs are finite; a program needn't handle non-finite values.
Results may differ from the reference program's by a relative error of at most 0.017.
Values may be sent and summed in bfloat16 or wider, within the bound.
A program may use at most 64 MiB of HBM per device.

```python
import jax
import jax.numpy as jnp
from jax import lax

C = 4096
M = 4096
GW = 64
ROW_DEV = 1
COLS = 256
GROUPS = 64
HEIGHT = 4
N_ROW = 4
N_CH = 8


def with_spikes(values, stream_key, source, target, blocks, factor):
    def block_of(axis_at):
        return (jnp.arange(values.shape[axis_at]) // (values.shape[axis_at] // blocks)).reshape((-1,) + (1,) * (values.ndim - 1 - axis_at))

    near = jax.random.permutation(stream_key, blocks)[block_of(target)]
    other_side = (block_of(target) + blocks // 2) % blocks
    return jnp.where((block_of(source) == near) | (block_of(source) == other_side), factor * values, values)


def shard_levels(stream_key, shape, pieces, smallest, top_value):
    gain = 1.0
    for position, parts in pieces:
        draws = jax.random.uniform(jax.random.fold_in(jax.random.fold_in(stream_key, 6), position), (parts,), jnp.float32, smallest / len(pieces), top_value / len(pieces))
        gain = gain * jnp.repeat(jnp.exp(draws), shape[position] // parts).reshape((-1,) + (1,) * (len(shape) - 1 - position))
    return gain


def bell_draw(own_key, extent, spread, limit, shards=(), kind=jnp.bfloat16):
    array = jax.random.normal(own_key, extent, jnp.float32) * spread
    if len(shards) > 0:
        array = shard_levels(own_key, extent, shards, -0.22, 0.18) * array
    return jnp.clip(array, min=-limit, max=limit).astype(kind)


def noise_with(stream_key, shape, scale, most, shards, heavy, kind=jnp.bfloat16):
    entries = scale * jax.random.normal(stream_key, shape, jnp.float32)
    if shards:
        entries = entries * shard_levels(stream_key, shape, shards, -0.22, 0.18)
    return jnp.clip(with_spikes(entries, jax.random.fold_in(stream_key, 3), *heavy), -most, most).astype(kind)


def setup_inputs(seed: int = 0) -> dict:
    streams_of = jax.random.split(jax.random.key(seed), 6)
    features = bell_draw(streams_of[0], (HEIGHT, COLS, C), 1.0, 6.0, ((0, 4), (2, 8)))
    w_in = noise_with(streams_of[1], (C, M), C ** -0.5, 0.125, ((1, 8),), (1, 0, 8, 2.0))
    w_group = bell_draw(streams_of[2], (3, 3, GW, M), (9 * GW) ** -0.5, 0.25, ((3, 8),))
    w_out = noise_with(streams_of[3], (M, C), M ** -0.5, 0.125, ((1, 8),), (1, 0, 8, 2.0))
    cotangent = bell_draw(streams_of[4], (HEIGHT, COLS, C), 1.0, 6.0, ((0, 4), (2, 8)))
    return {"features": features, "w_in": w_in, "w_group": w_group, "w_out": w_out, "cotangent": cotangent}


def silu_slope(values):
    sigma = jax.nn.sigmoid(values)
    return sigma * (1.0 + values * (1.0 - sigma))


def round_keep(values):
    rounded = lax.optimization_barrier(values.astype(jnp.bfloat16))
    return rounded.astype(jnp.float32)


def block_partials(left, right, blocks):
    pixel_count = left.shape[0]
    other_count = right.shape[0]
    left_blocks = left.reshape(pixel_count, blocks, -1).transpose(1, 0, 2)
    right_blocks = right.reshape(other_count, blocks, -1).transpose(1, 0, 2)

    def add_block(total, pair):
        piece = jnp.dot(pair[0], pair[1].T, preferred_element_type=jnp.float32)
        return total + round_keep(piece), None

    start_total = jnp.zeros((pixel_count, other_count), jnp.float32)
    total, unused = lax.scan(add_block, start_total, (left_blocks, right_blocks))
    return total


def group_forward(padded, taps, height, breadth):
    total = jnp.zeros((height, breadth, padded.shape[2], padded.shape[3]), jnp.float32)
    for row_tap in range(3):
        for col_tap in range(3):
            window = padded[row_tap:row_tap + height, col_tap:col_tap + breadth]
            total = total + jnp.einsum("rcgi,igj->rcgj", window, taps[row_tap, col_tap])
    return total


def group_backward(padded, taps, height, breadth):
    total = jnp.zeros((height, breadth, padded.shape[2], padded.shape[3]), jnp.float32)
    for row_tap in range(3):
        for col_tap in range(3):
            window = padded[2 - row_tap:2 - row_tap + height, 2 - col_tap:2 - col_tap + breadth]
            total = total + jnp.einsum("rcgj,igj->rcgi", window, taps[row_tap, col_tap])
    return total


def group_weight(padded, grads, height, breadth):
    rows_of_taps = []
    for row_tap in range(3):
        line = []
        for col_tap in range(3):
            window = padded[row_tap:row_tap + height, col_tap:col_tap + breadth]
            line.append(jnp.einsum("rcgi,rcgj->igj", window, grads))
        rows_of_taps.append(jnp.stack(line))
    return jnp.stack(rows_of_taps)


def reference(features, w_in, w_group, w_out, cotangent):
    height = ROW_DEV * N_ROW
    breadth = COLS
    pixel_count = height * breadth
    flat_in = features.reshape(pixel_count, C)
    pre_one = jnp.dot(flat_in, w_in, preferred_element_type=jnp.float32)
    act_one = jax.nn.silu(pre_one).astype(jnp.bfloat16)
    taps = w_group.astype(jnp.float32).reshape(3, 3, GW, GROUPS, GW)
    edge = ((1, 1), (1, 1), (0, 0), (0, 0))
    padded_one = jnp.pad(act_one.reshape(height, breadth, GROUPS, GW).astype(jnp.float32), edge)
    pre_two = group_forward(padded_one, taps, height, breadth).reshape(pixel_count, M)
    act_two = jax.nn.silu(pre_two).astype(jnp.bfloat16)
    branch = jnp.dot(act_two, w_out, preferred_element_type=jnp.float32)
    block_out = (flat_in.astype(jnp.float32) + branch).astype(jnp.bfloat16).reshape(height, breadth, C)
    grad_flat = cotangent.reshape(pixel_count, C)
    d_two = block_partials(grad_flat, w_out, N_CH)
    grad_two = (d_two * silu_slope(pre_two)).astype(jnp.bfloat16)
    padded_two = jnp.pad(grad_two.reshape(height, breadth, GROUPS, GW).astype(jnp.float32), edge)
    d_one = group_backward(padded_two, taps, height, breadth).reshape(pixel_count, M)
    grad_one = (d_one * silu_slope(pre_one)).astype(jnp.bfloat16)
    d_input = block_partials(grad_one, w_in, N_CH)
    grad_input = (grad_flat.astype(jnp.float32) + d_input).astype(jnp.bfloat16).reshape(height, breadth, C)
    band = ROW_DEV * breadth

    def add_band(totals, index):
        first = (index * band).astype(jnp.int32)
        in_band = lax.dynamic_slice_in_dim(flat_in, first, band, 0)
        one_band = lax.dynamic_slice_in_dim(grad_one, first, band, 0)
        mid_band = lax.dynamic_slice_in_dim(act_two, first, band, 0)
        cot_band = lax.dynamic_slice_in_dim(grad_flat, first, band, 0)
        in_part = jnp.dot(in_band.T, one_band, preferred_element_type=jnp.float32)
        out_part = jnp.dot(mid_band.T, cot_band, preferred_element_type=jnp.float32)
        top_row = (index * ROW_DEV).astype(jnp.int32)
        pad_band = lax.dynamic_slice_in_dim(padded_one, top_row, ROW_DEV + 2, 0)
        two_band = lax.dynamic_slice_in_dim(grad_two, first, band, 0)
        two_band = two_band.reshape(ROW_DEV, breadth, GROUPS, GW).astype(jnp.float32)
        group_part = group_weight(pad_band, two_band, ROW_DEV, breadth).reshape(3, 3, GW, M)
        return (totals[0] + round_keep(in_part), totals[1] + round_keep(out_part), totals[2] + round_keep(group_part)), None

    start_totals = (jnp.zeros((C, M), jnp.float32), jnp.zeros((M, C), jnp.float32), jnp.zeros((3, 3, GW, M), jnp.float32))
    totals, unused = lax.scan(add_band, start_totals, jnp.arange(N_ROW, dtype=jnp.int32))
    return (block_out, grad_input, totals[0].astype(jnp.bfloat16), totals[2].astype(jnp.bfloat16), totals[1].astype(jnp.bfloat16))
```

```python
import jax
import jax.numpy as jnp
from jax import lax
from jax.sharding import PartitionSpec as P


GATHER_BYTES = 8 * 1024 * 1024


def padded_2(cells, sides, width):
    for axis, dim in sides:
        count = lax.axis_size(axis)
        ends = count - 1
        head = lax.slice_in_dim(cells, 0, width, axis=dim)
        tail = lax.slice_in_dim(cells, cells.shape[dim] - width, cells.shape[dim], axis=dim)
        cells = jnp.concatenate(
            [
                lax.ppermute(tail, axis, [(i, (i + 1) % count) for i in range(ends)]),
                cells,
                lax.ppermute(head, axis, [((i + 1) % count, i) for i in range(ends)]),
            ],
            axis=dim,
        )
    return cells


def silu_slope(values):
    sigma = jax.nn.sigmoid(values)
    return sigma * (1.0 + values * (1.0 - sigma))


def full_channels(local):
    return lax.all_gather(local, "ch", axis=2, tiled=True)


def row_rims(local):
    padded = padded_2(local, (("row", 0),), 1)
    return jnp.pad(padded, ((0, 0), (1, 1), (0, 0)))


def group_view(local, group_width):
    return local.reshape(local.shape[0], local.shape[1], local.shape[2] // group_width, group_width)


def body(features, w_in, w_group, w_out, cotangent):
    row_count, col_count, local_ch = features.shape
    group_width = w_group.shape[2]
    local_mid = w_in.shape[1]
    pixel_count = row_count * col_count
    gathered = full_channels(features)
    flat_in = gathered.reshape(pixel_count, -1)
    pre_one = jnp.dot(flat_in, w_in, preferred_element_type=jnp.float32)
    act_one = jax.nn.silu(pre_one).astype(jnp.bfloat16).reshape(row_count, col_count, local_mid)
    padded_one = group_view(row_rims(act_one), group_width)
    filters = w_group.reshape(3, 3, group_width, local_mid // group_width, group_width)
    pre_two = jnp.zeros((row_count, col_count, local_mid // group_width, group_width), jnp.float32)
    for row_tap in range(3):
        for col_tap in range(3):
            window = padded_one[row_tap : row_tap + row_count, col_tap : col_tap + col_count]
            pre_two = pre_two + jnp.einsum(
                "rcgi,igj->rcgj",
                window,
                filters[row_tap, col_tap],
                preferred_element_type=jnp.float32,
            )
    pre_two = pre_two.reshape(pixel_count, local_mid)
    act_two = jax.nn.silu(pre_two).astype(jnp.bfloat16)
    mid_full = full_channels(act_two.reshape(row_count, col_count, local_mid)).reshape(
        pixel_count, -1
    )
    branch = jnp.dot(mid_full, w_out, preferred_element_type=jnp.float32)
    flat_local = features.reshape(pixel_count, local_ch)
    block_out = (
        (flat_local.astype(jnp.float32) + branch)
        .astype(jnp.bfloat16)
        .reshape(row_count, col_count, local_ch)
    )
    grad_flat = cotangent.reshape(pixel_count, local_ch)
    partial = lax.dot_general(
        w_out, grad_flat, (((1,), (1,)), ((), ())), preferred_element_type=jnp.float32
    ).astype(jnp.bfloat16)
    d_two = (
        lax.psum_scatter(partial, "ch", scatter_dimension=0, tiled=True).astype(jnp.float32).T
    )
    grad_two = (d_two * silu_slope(pre_two)).astype(jnp.bfloat16)
    padded_two = group_view(
        row_rims(grad_two.reshape(row_count, col_count, local_mid)), group_width
    )
    d_one = jnp.zeros((row_count, col_count, local_mid // group_width, group_width), jnp.float32)
    for row_tap in range(3):
        for col_tap in range(3):
            window = padded_two[
                2 - row_tap : 2 - row_tap + row_count, 2 - col_tap : 2 - col_tap + col_count
            ]
            d_one = d_one + jnp.einsum(
                "rcgj,igj->rcgi",
                window,
                filters[row_tap, col_tap],
                preferred_element_type=jnp.float32,
            )
    grad_one = (d_one.reshape(pixel_count, local_mid) * silu_slope(pre_one)).astype(jnp.bfloat16)
    grad_view = group_view(grad_two.reshape(row_count, col_count, local_mid), group_width)
    tap_rows = []
    for row_tap in range(3):
        tap_line = []
        for col_tap in range(3):
            window = padded_one[row_tap : row_tap + row_count, col_tap : col_tap + col_count]
            tap_line.append(
                jnp.einsum("rcgi,rcgj->igj", window, grad_view, preferred_element_type=jnp.float32)
            )
        tap_rows.append(jnp.stack(tap_line))
    group_grad = jnp.stack(tap_rows).reshape(3, 3, group_width, local_mid)
    rows = lax.axis_size("row")
    spread = rows * flat_in.size * flat_in.dtype.itemsize <= GATHER_BYTES
    left_in, right_in, left_out, right_out = flat_in, grad_one, mid_full, grad_flat
    if spread:
        left_in, right_in, left_out, right_out = (
            lax.all_gather(v, "row", axis=0, tiled=True)
            for v in (flat_in, grad_one, mid_full, grad_flat)
        )
    in_grad = lax.dot_general(
        left_in, right_in, (((0,), (0,)), ((), ())), preferred_element_type=jnp.float32
    ).astype(jnp.bfloat16)
    out_grad = lax.dot_general(
        left_out, right_out, (((0,), (0,)), ((), ())), preferred_element_type=jnp.float32
    ).astype(jnp.bfloat16)
    if not spread:
        in_grad, out_grad = lax.psum((in_grad, out_grad), "row")
    d_input = (
        lax.psum_scatter(
            lax.dot_general(
                w_in, grad_one, (((1,), (1,)), ((), ())), preferred_element_type=jnp.float32
            ).astype(jnp.bfloat16),
            "ch",
            scatter_dimension=0,
            tiled=True,
        )
        .astype(jnp.float32)
        .T
    )
    grad_input = (
        (grad_flat.astype(jnp.float32) + d_input)
        .astype(jnp.bfloat16)
        .reshape(row_count, col_count, local_ch)
    )
    group_grad = lax.psum(group_grad.astype(jnp.bfloat16), "row")
    return block_out, grad_input, in_grad, group_grad, out_grad


def solution(mesh):
    placed = (
        P("row", None, "ch"),
        P(None, "ch"),
        P(None, None, None, "ch"),
        P(None, "ch"),
        P("row", None, "ch"),
    )
    return jax.shard_map(
        body,
        mesh=mesh,
        in_specs=placed,
        out_specs=(
            P("row", None, "ch"),
            P("row", None, "ch"),
            P(None, "ch"),
            P(None, None, None, "ch"),
            P(None, "ch"),
        ),
        check_vma=False,
    )
```

```python
import jax
import jax.numpy as jnp
from jax import lax
from jax.experimental import pallas as pl
from jax.experimental.pallas import tpu as pltpu
from jax.sharding import PartitionSpec as P


GATHER_BYTES = 8 * 1024 * 1024
MESH = pl.DeviceIdType.MESH
BF = jnp.bfloat16
F32 = jnp.float32


def padded_2(cells, sides, width):
    for axis, dim in sides:
        count = lax.axis_size(axis)
        ends = count - 1
        head = lax.slice_in_dim(cells, 0, width, axis=dim)
        tail = lax.slice_in_dim(cells, cells.shape[dim] - width, cells.shape[dim], axis=dim)
        cells = jnp.concatenate(
            [
                lax.ppermute(tail, axis, [(i, (i + 1) % count) for i in range(ends)]),
                cells,
                lax.ppermute(head, axis, [((i + 1) % count, i) for i in range(ends)]),
            ],
            axis=dim,
        )
    return cells


def silu_slope(values):
    sigma = jax.nn.sigmoid(values)
    return sigma * (1.0 + values * (1.0 - sigma))


def full_channels(local):
    return lax.all_gather(local, "ch", axis=2, tiled=True)


def row_rims(local):
    padded = padded_2(local, (("row", 0),), 1)
    return jnp.pad(padded, ((0, 0), (1, 1), (0, 0)))


def group_view(local, group_width):
    return local.reshape(local.shape[0], local.shape[1], local.shape[2] // group_width, group_width)


def wide_body(features, w_in, w_group, w_out, cotangent):
    row_count, col_count, local_ch = features.shape
    group_width = w_group.shape[2]
    local_mid = w_in.shape[1]
    pixel_count = row_count * col_count
    gathered = full_channels(features)
    flat_in = gathered.reshape(pixel_count, -1)
    pre_one = jnp.dot(flat_in, w_in, preferred_element_type=jnp.float32)
    act_one = jax.nn.silu(pre_one).astype(jnp.bfloat16).reshape(row_count, col_count, local_mid)
    padded_one = group_view(row_rims(act_one), group_width)
    filters = w_group.reshape(3, 3, group_width, local_mid // group_width, group_width)
    pre_two = jnp.zeros((row_count, col_count, local_mid // group_width, group_width), jnp.float32)
    for row_tap in range(3):
        for col_tap in range(3):
            window = padded_one[row_tap : row_tap + row_count, col_tap : col_tap + col_count]
            pre_two = pre_two + jnp.einsum(
                "rcgi,igj->rcgj",
                window,
                filters[row_tap, col_tap],
                preferred_element_type=jnp.float32,
            )
    pre_two = pre_two.reshape(pixel_count, local_mid)
    act_two = jax.nn.silu(pre_two).astype(jnp.bfloat16)
    mid_full = full_channels(act_two.reshape(row_count, col_count, local_mid)).reshape(
        pixel_count, -1
    )
    branch = jnp.dot(mid_full, w_out, preferred_element_type=jnp.float32)
    flat_local = features.reshape(pixel_count, local_ch)
    block_out = (
        (flat_local.astype(jnp.float32) + branch)
        .astype(jnp.bfloat16)
        .reshape(row_count, col_count, local_ch)
    )
    grad_flat = cotangent.reshape(pixel_count, local_ch)
    partial = lax.dot_general(
        w_out, grad_flat, (((1,), (1,)), ((), ())), preferred_element_type=jnp.float32
    ).astype(jnp.bfloat16)
    d_two = (
        lax.psum_scatter(partial, "ch", scatter_dimension=0, tiled=True).astype(jnp.float32).T
    )
    grad_two = (d_two * silu_slope(pre_two)).astype(jnp.bfloat16)
    padded_two = group_view(
        row_rims(grad_two.reshape(row_count, col_count, local_mid)), group_width
    )
    d_one = jnp.zeros((row_count, col_count, local_mid // group_width, group_width), jnp.float32)
    for row_tap in range(3):
        for col_tap in range(3):
            window = padded_two[
                2 - row_tap : 2 - row_tap + row_count, 2 - col_tap : 2 - col_tap + col_count
            ]
            d_one = d_one + jnp.einsum(
                "rcgj,igj->rcgi",
                window,
                filters[row_tap, col_tap],
                preferred_element_type=jnp.float32,
            )
    grad_one = (d_one.reshape(pixel_count, local_mid) * silu_slope(pre_one)).astype(jnp.bfloat16)
    grad_view = group_view(grad_two.reshape(row_count, col_count, local_mid), group_width)
    tap_rows = []
    for row_tap in range(3):
        tap_line = []
        for col_tap in range(3):
            window = padded_one[row_tap : row_tap + row_count, col_tap : col_tap + col_count]
            tap_line.append(
                jnp.einsum("rcgi,rcgj->igj", window, grad_view, preferred_element_type=jnp.float32)
            )
        tap_rows.append(jnp.stack(tap_line))
    group_grad = jnp.stack(tap_rows).reshape(3, 3, group_width, local_mid)
    rows = lax.axis_size("row")
    spread = rows * flat_in.size * flat_in.dtype.itemsize <= GATHER_BYTES
    left_in, right_in, left_out, right_out = flat_in, grad_one, mid_full, grad_flat
    if spread:
        left_in, right_in, left_out, right_out = (
            lax.all_gather(v, "row", axis=0, tiled=True)
            for v in (flat_in, grad_one, mid_full, grad_flat)
        )
    in_grad = lax.dot_general(
        left_in, right_in, (((0,), (0,)), ((), ())), preferred_element_type=jnp.float32
    ).astype(jnp.bfloat16)
    out_grad = lax.dot_general(
        left_out, right_out, (((0,), (0,)), ((), ())), preferred_element_type=jnp.float32
    ).astype(jnp.bfloat16)
    if not spread:
        in_grad, out_grad = lax.psum((in_grad, out_grad), "row")
    d_input = (
        lax.psum_scatter(
            lax.dot_general(
                w_in, grad_one, (((1,), (1,)), ((), ())), preferred_element_type=jnp.float32
            ).astype(jnp.bfloat16),
            "ch",
            scatter_dimension=0,
            tiled=True,
        )
        .astype(jnp.float32)
        .T
    )
    grad_input = (
        (grad_flat.astype(jnp.float32) + d_input)
        .astype(jnp.bfloat16)
        .reshape(row_count, col_count, local_ch)
    )
    group_grad = lax.psum(group_grad.astype(jnp.bfloat16), "row")
    return block_out, grad_input, in_grad, group_grad, out_grad


def dot(a, b):
    return jnp.dot(a, b, preferred_element_type=F32)


def dot_nt(a, b):
    return lax.dot_general(a, b, (((1,), (1,)), ((), ())), preferred_element_type=F32)


def dot_tn(a, b):
    return lax.dot_general(a, b, (((0,), (0,)), ((), ())), preferred_element_type=F32)


def moved(values, step):
    count = values.shape[0]
    at = lax.broadcasted_iota(jnp.int32, values.shape, 0)
    edge = 0 if step == 1 else count - 1
    return jnp.where(at == edge, 0.0, pltpu.roll(values, step % count, 0))


class Fabric:
    def __init__(self):
        self.row = lax.axis_index("row")
        self.ch = lax.axis_index("ch")
        self.core = lax.rem(self.ch, 2)
        self.z = self.ch // 2
        self.zs = lax.axis_size("ch") // 2
        x, y = lax.rem(self.row, 2), self.row // 2
        self.row_x = y * 2 + (1 - x)
        self.row_y = (1 - y) * 2 + x
        self.row_d = (1 - y) * 2 + (1 - x)
        self.twin = self.z * 2 + (1 - self.core)
        self.sent = []

    def z_at(self, d):
        return lax.rem(self.z + d, self.zs)

    def ch_at(self, d):
        return self.z_at(d) * 2 + self.core

    def partners(self):
        out = [(self.row, self.ch_at(d)) for d in range(1, self.zs)]
        out += [(r, self.ch) for r in (self.row_x, self.row_y, self.row_d)]
        return out + [(self.row, self.twin)]

    def send(self, src, dst, send_sem, recv_sem, device):
        copy = pltpu.make_async_remote_copy(
            src_ref=src,
            dst_ref=dst,
            send_sem=send_sem,
            recv_sem=recv_sem,
            device_id=device,
            device_id_type=MESH,
        )
        copy.start()
        self.sent.append(copy)

    def arrived(self, dst, sem):
        pltpu.make_async_remote_copy(
            src_ref=dst,
            dst_ref=dst,
            send_sem=sem,
            recv_sem=sem,
            device_id=(self.row, self.twin),
            device_id_type=MESH,
        ).wait_recv()


class Gather:
    def __init__(self, fab, buf, recv, send_z, send_x, send_y, send_t):
        self.fab, self.buf, self.recv = fab, buf, recv
        self.send_z, self.send_x, self.send_y, self.send_t = send_z, send_x, send_y, send_t

    def push(self, k, r, send_sem, device):
        slot = self.buf.at[k, r]
        self.fab.send(slot, slot, send_sem, self.recv.at[k, r], device)

    def to_x(self, k, r, n):
        self.push(k, r, self.send_x.at[n], (self.fab.row_x, self.fab.ch))

    def to_y(self, k, r, n):
        self.push(k, r, self.send_y.at[n], (self.fab.row_y, self.fab.ch))

    def to_twin(self, k, r, n):
        self.push(k, r, self.send_t.at[n], (self.fab.row, self.fab.twin))

    def wait(self, k, r):
        self.fab.arrived(self.buf.at[k, r], self.recv.at[k, r])

    def start(self):
        f = self.fab
        for d in range(1, f.zs):
            self.push(f.ch, f.row, self.send_z.at[d - 1], (f.row, f.ch_at(d)))
        self.to_x(f.ch, f.row, 0)
        self.to_y(f.ch, f.row, 0)
        self.to_twin(f.ch, f.row, 0)

    def pump_z(self):
        f = self.fab
        for d in range(1, f.zs):
            k = f.ch_at(d)
            self.wait(k, f.row)
            self.to_x(k, f.row, d)
            self.to_y(k, f.row, d)
            self.to_twin(k, f.row, d)

    def pump_xy(self):
        f = self.fab
        half = f.zs // 2
        for d in range(f.zs):
            k = f.ch_at(d)
            self.wait(k, f.row_x)
            if d < half:
                self.to_y(k, f.row_x, f.zs + d)
            self.to_twin(k, f.row_x, f.zs + d)
            self.wait(k, f.row_y)
            if d >= half:
                self.to_x(k, f.row_y, f.zs + d - half)
            self.to_twin(k, f.row_y, 2 * f.zs + d)

    def pump_d(self):
        f = self.fab
        for d in range(f.zs):
            k = f.ch_at(d)
            self.wait(k, f.row_d)
            self.to_twin(k, f.row_d, 3 * f.zs + d)

    def twin_row(self, r):
        f = self.fab
        for d in range(f.zs):
            self.wait(f.z_at(d) * 2 + (1 - f.core), r)


class Scatter:
    def __init__(self, fab, give, got, out, far, acc, give_s, got_s, out_s, far_s):
        self.fab, self.give, self.got, self.out, self.far, self.acc = fab, give, got, out, far, acc
        self.give_s, self.got_s, self.out_s, self.far_s = give_s, got_s, out_s, far_s

    def part(self, lhs, w_ref, k):
        width = lhs.shape[1]
        rows = pl.ds(pl.multiple_of(k * width, width), width)
        return dot_nt(lhs, w_ref[rows, :])

    def start(self, lhs, w_ref):
        f = self.fab
        for d in (1, 2, 3, 0):
            at = f.z_at(d)
            self.give[at] = self.part(lhs, w_ref, at * 2 + (1 - f.core)).astype(BF)
            f.send(
                self.give.at[at],
                self.got.at[at],
                self.give_s.at[d],
                self.got_s.at[at],
                (f.row, f.twin),
            )

    def middle(self, lhs, w_ref):
        f = self.fab
        for d in (1, 2, 3, 0):
            at = f.z_at(d)
            own = self.part(lhs, w_ref, at * 2 + f.core)
            f.arrived(self.got.at[at], self.got_s.at[at])
            own = own + self.got[at].astype(F32)
            if d == 0:
                self.acc[...] = own
            else:
                self.out[at] = own.astype(BF)
                f.send(
                    self.out.at[at],
                    self.far.at[f.z],
                    self.out_s.at[d - 1],
                    self.far_s.at[f.z],
                    (f.row, f.ch_at(d)),
                )

    def finish(self):
        f = self.fab
        for d in (1, 2, 3):
            at = f.z_at(d)
            f.arrived(self.far.at[at], self.far_s.at[at])
        total = self.acc[...]
        for d in (1, 2, 3):
            total = total + self.far[f.z_at(d)].astype(F32)
        return total


def block_kernel(*refs):
    (feat, w_in_hbm, wg, w_out_hbm, cot, out, g_in, gw_in, gw_group, gw_out) = refs[:10]
    (b1, b2, w_in, w_out, pre, act, gt, g1, cots, shifted, wide, stage) = refs[10:22]
    (r1, z1, x1, y1, t1, r2, z2, x2, y2, t2) = refs[22:32]
    s1, s2 = refs[32:41], refs[41:50]
    cot_send, cot_recv, gt_send, gt_recv, local = refs[50:55]
    fab = Fabric()
    rows = cots.shape[0]
    pixels, width = feat.shape
    chunk = wide.shape[2]
    gw = wg.shape[1]
    count_k = b1.shape[0]
    chunks = [slice(i * chunk, (i + 1) * chunk) for i in range(width // chunk)]

    load_out = pltpu.make_async_copy(w_out_hbm, w_out, local.at[0])
    load_in = pltpu.make_async_copy(w_in_hbm, w_in, local.at[1])
    load_out.start()
    load_in.start()
    barrier = pltpu.get_barrier_semaphore()
    partners = fab.partners()
    for device in partners:
        pl.semaphore_signal(barrier, inc=1, device_id=device, device_id_type=MESH)
    pl.semaphore_wait(barrier, len(partners))

    gather1 = Gather(fab, b1, r1, z1, x1, y1, t1)
    gather2 = Gather(fab, b2, r2, z2, x2, y2, t2)
    scatter1 = Scatter(fab, *s1)
    scatter2 = Scatter(fab, *s2)
    other_rows = (fab.row_x, fab.row_y, fab.row_d)

    b1[fab.ch, fab.row] = feat[...]
    gather1.start()
    cots[fab.row] = cot[...]
    load_out.wait()
    scatter1.start(cot[...], w_out)

    blank = jnp.zeros((pixels, width), BF)
    act[0] = blank
    act[rows + 1] = blank
    gt[0] = blank
    gt[rows + 1] = blank
    row_group = lax.broadcasted_iota(jnp.int32, (chunk, chunk), 0) // gw
    col_group = lax.broadcasted_iota(jnp.int32, (chunk, chunk), 1) // gw
    same = row_group == col_group

    def widen(tap, carry):
        for i, part in enumerate(chunks):
            taps = wg[tap, :, part].astype(F32)
            dense = jnp.concatenate([taps] * (chunk // gw), axis=0)
            wide[tap, i] = jnp.where(same, dense, 0.0).astype(BF)
        return carry

    lax.fori_loop(0, 9, widen, 0)

    scatter1.middle(cot[...], w_out)
    gather1.pump_z()
    for n, r in enumerate(other_rows):
        fab.send(
            cots.at[fab.row],
            cots.at[fab.row],
            cot_send.at[n],
            cot_recv.at[fab.row],
            (r, fab.ch),
        )
    load_in.wait()

    def first(r):
        gather1.twin_row(r)
        pre[r] = jnp.zeros((pixels, width), F32)

        def add(k, carry):
            lines = pl.ds(pl.multiple_of(k * width, width), width)
            pre[r] += dot(b1[k, r], w_in[lines, :])
            return carry

        lax.fori_loop(0, count_k, add, 0)
        value = pre[r]
        act[r + 1] = (value * jax.nn.sigmoid(value)).astype(BF)

    first(fab.row)
    gather1.pump_xy()
    first(fab.row_x)
    gather1.pump_d()
    first(fab.row_d)
    first(fab.row_y)

    taps_of = [[a * 3 + b for a in range(3)] for b in range(3)]
    two = []
    for i, part in enumerate(chunks):
        total = None
        for b in range(3):
            side = None
            for a in range(3):
                term = dot(act[fab.row + a, :, part], wide[taps_of[b][a], i])
                side = term if side is None else side + term
            side = moved(side, 1) if b == 0 else moved(side, -1) if b == 2 else side
            total = side if total is None else total + side
        two.append(total)
    slopes = []
    for i, part in enumerate(chunks):
        b2[fab.ch, fab.row, :, part] = (two[i] * jax.nn.sigmoid(two[i])).astype(BF)
        slopes.append(silu_slope(two[i]))
    gather2.start()
    d_two = scatter1.finish()
    for i, part in enumerate(chunks):
        gt[fab.row + 1, :, part] = (d_two[:, part] * slopes[i]).astype(BF)
    for n, r in enumerate(other_rows):
        fab.send(
            gt.at[fab.row + 1],
            gt.at[fab.row + 1],
            gt_send.at[n],
            gt_recv.at[fab.row],
            (r, fab.ch),
        )
    gather2.pump_z()
    for r in other_rows:
        fab.arrived(gt.at[r + 1], gt_recv.at[r])

    def back(q, carry):
        for i, part in enumerate(chunks):
            total = None
            for b in range(3):
                side = None
                for a in range(3):
                    term = dot_nt(gt[q + 2 - a, :, part], wide[taps_of[b][a], i])
                    side = term if side is None else side + term
                side = moved(side, -1) if b == 0 else moved(side, 1) if b == 2 else side
                total = side if total is None else total + side
            g1[q, :, part] = (total * silu_slope(pre[q, :, part])).astype(BF)
        return carry

    lax.fori_loop(0, rows, back, 0)
    scatter2.start(g1[fab.row], w_in)
    scatter2.middle(g1[fab.row], w_in)
    gather2.pump_xy()

    gather2.twin_row(fab.row)
    pre[0] = feat[...].astype(F32)

    def last(k, carry):
        lines = pl.ds(pl.multiple_of(k * width, width), width)
        pre[0] += dot(b2[k, fab.row], w_out[lines, :])
        return carry

    lax.fori_loop(0, count_k, last, 0)
    out[...] = pre[0].astype(BF)

    def weight_grad(left, right, result, sems):
        def store(k, slot):
            return pltpu.make_async_copy(
                stage.at[slot],
                result.at[pl.ds(pl.multiple_of(k * width, width), width), :],
                sems.at[slot],
            )

        def step(pair, carry):
            for slot in range(2):
                k = pair * 2 + slot

                @pl.when(pair > 0)
                def _():
                    store(k - 2, slot).wait()

                lhs = left[k].reshape(rows * pixels, width)
                stage[slot] = dot_tn(lhs, right[...].reshape(rows * pixels, width)).astype(BF)
                store(k, slot).start()
            return carry

        lax.fori_loop(0, count_k // 2, step, 0)
        for slot in range(2):
            store(count_k - 2 + slot, slot).wait()

    weight_grad(b1, g1, gw_in, local.at[pl.ds(2, 2)])
    gather2.pump_d()

    for b in range(3):

        def move(q, carry):
            value = gt[q + 1].astype(F32)
            value = moved(value, -1) if b == 0 else moved(value, 1) if b == 2 else value
            shifted[q] = value.astype(BF)
            return carry

        lax.fori_loop(0, rows, move, 0)

        def tap_grad(a, carry):
            for part in chunks:
                lhs = act[pl.ds(a, rows), :, part].reshape(rows * pixels, chunk)
                full = dot_tn(lhs, shifted[:, :, part].reshape(rows * pixels, chunk))
                full = jnp.where(same, full, 0.0).reshape(chunk // gw, gw, chunk)
                gw_group[a * 3 + b, :, part] = jnp.sum(full, axis=0).astype(BF)
            return carry

        lax.fori_loop(0, 3, tap_grad, 0)

    g_in[...] = (cot[...].astype(F32) + scatter2.finish()).astype(BF)
    for r in other_rows:
        fab.arrived(cots.at[r], cot_recv.at[r])
        gather2.twin_row(r)
    weight_grad(b2, cots, gw_out, local.at[pl.ds(4, 2)])
    for copy in fab.sent:
        copy.wait_send()


def body(features, w_in, w_group, w_out, cotangent):
    row_count, pixels, width = features.shape
    rows, lanes = lax.axis_size("row"), lax.axis_size("ch")
    total = rows * lanes * features.size * features.dtype.itemsize
    fits = (rows, lanes, row_count) == (4, 8, 1) and w_in.shape[1] == width == 512
    if not fits or total > GATHER_BYTES:
        return wide_body(features, w_in, w_group, w_out, cotangent)
    zs = lanes // 2
    channels = w_in.shape[0]
    gw = w_group.shape[2]
    dma = pltpu.SemaphoreType.DMA
    vmem = pltpu.VMEM
    gather_sems = [dma((lanes, rows)), dma((zs - 1,)), dma((6,)), dma((6,)), dma((rows * zs,))]
    part = vmem((zs, pixels, width), BF)
    scatter = [part, part, part, part, vmem((pixels, width), F32)]
    scatter += [dma((zs,)), dma((zs,)), dma((zs - 1,)), dma((zs,))]
    scratch = [
        vmem((lanes, rows, pixels, width), BF),
        vmem((lanes, rows, pixels, width), BF),
        vmem((channels, width), BF),
        vmem((channels, width), BF),
        vmem((rows, pixels, width), F32),
        vmem((rows + 2, pixels, width), BF),
        vmem((rows + 2, pixels, width), BF),
        vmem((rows, pixels, width), BF),
        vmem((rows, pixels, width), BF),
        vmem((rows, pixels, width), BF),
        vmem((9, width // 256, 256, 256), BF),
        vmem((2, width, width), BF),
    ]
    scratch += gather_sems * 2 + scatter * 2
    scratch += [dma((3,)), dma((rows,)), dma((3,)), dma((rows,)), dma((6,))]
    in_vmem = pl.BlockSpec(memory_space=pltpu.VMEM)
    in_any = pl.BlockSpec(memory_space=pl.ANY)
    flat = jax.ShapeDtypeStruct((pixels, width), BF)
    weight = jax.ShapeDtypeStruct((channels, width), BF)
    out, g_in, gw_in, gw_group, gw_out = pl.pallas_call(
        block_kernel,
        out_shape=[flat, flat, weight, jax.ShapeDtypeStruct((9, gw, width), BF), weight],
        in_specs=[in_vmem, in_any, in_vmem, in_any, in_vmem],
        out_specs=[in_vmem, in_vmem, in_any, in_vmem, in_any],
        scratch_shapes=scratch,
        compiler_params=pltpu.CompilerParams(
            collective_id=0, has_side_effects=True, vmem_limit_bytes=60 * 1024 * 1024
        ),
    )(
        features.reshape(pixels, width),
        w_in,
        w_group.reshape(9, gw, width),
        w_out,
        cotangent.reshape(pixels, width),
    )
    return (
        out.reshape(features.shape),
        g_in.reshape(features.shape),
        gw_in,
        gw_group.reshape(w_group.shape),
        gw_out,
    )


def solution(mesh):
    placed = (
        P("row", None, "ch"),
        P(None, "ch"),
        P(None, None, None, "ch"),
        P(None, "ch"),
        P("row", None, "ch"),
    )
    return jax.shard_map(
        body,
        mesh=mesh,
        in_specs=placed,
        out_specs=(
            P("row", None, "ch"),
            P("row", None, "ch"),
            P(None, "ch"),
            P(None, None, None, "ch"),
            P(None, "ch"),
        ),
        check_vma=False,
    )
```

```python
import jax
import jax.numpy as jnp
from jax import lax
from jax.experimental import pallas as pl
from jax.experimental.pallas import tpu as pltpu
from jax.sharding import PartitionSpec as P


GATHER_BYTES = 8 * 1024 * 1024
MESH = pl.DeviceIdType.MESH
BF = jnp.bfloat16
F32 = jnp.float32


def padded_2(cells, sides, width):
    for axis, dim in sides:
        count = lax.axis_size(axis)
        ends = count - 1
        head = lax.slice_in_dim(cells, 0, width, axis=dim)
        tail = lax.slice_in_dim(cells, cells.shape[dim] - width, cells.shape[dim], axis=dim)
        cells = jnp.concatenate(
            [
                lax.ppermute(tail, axis, [(i, (i + 1) % count) for i in range(ends)]),
                cells,
                lax.ppermute(head, axis, [((i + 1) % count, i) for i in range(ends)]),
            ],
            axis=dim,
        )
    return cells


def silu_slope(values):
    sigma = jax.nn.sigmoid(values)
    return sigma * (1.0 + values * (1.0 - sigma))


def full_channels(local):
    return lax.all_gather(local, "ch", axis=2, tiled=True)


def row_rims(local):
    padded = padded_2(local, (("row", 0),), 1)
    return jnp.pad(padded, ((0, 0), (1, 1), (0, 0)))


def group_view(local, group_width):
    return local.reshape(local.shape[0], local.shape[1], local.shape[2] // group_width, group_width)


def wide_body(features, w_in, w_group, w_out, cotangent):
    row_count, col_count, local_ch = features.shape
    group_width = w_group.shape[2]
    local_mid = w_in.shape[1]
    pixel_count = row_count * col_count
    gathered = full_channels(features)
    flat_in = gathered.reshape(pixel_count, -1)
    pre_one = jnp.dot(flat_in, w_in, preferred_element_type=jnp.float32)
    act_one = jax.nn.silu(pre_one).astype(jnp.bfloat16).reshape(row_count, col_count, local_mid)
    padded_one = group_view(row_rims(act_one), group_width)
    filters = w_group.reshape(3, 3, group_width, local_mid // group_width, group_width)
    pre_two = jnp.zeros((row_count, col_count, local_mid // group_width, group_width), jnp.float32)
    for row_tap in range(3):
        for col_tap in range(3):
            window = padded_one[row_tap : row_tap + row_count, col_tap : col_tap + col_count]
            pre_two = pre_two + jnp.einsum(
                "rcgi,igj->rcgj",
                window,
                filters[row_tap, col_tap],
                preferred_element_type=jnp.float32,
            )
    pre_two = pre_two.reshape(pixel_count, local_mid)
    act_two = jax.nn.silu(pre_two).astype(jnp.bfloat16)
    mid_full = full_channels(act_two.reshape(row_count, col_count, local_mid)).reshape(
        pixel_count, -1
    )
    branch = jnp.dot(mid_full, w_out, preferred_element_type=jnp.float32)
    flat_local = features.reshape(pixel_count, local_ch)
    block_out = (
        (flat_local.astype(jnp.float32) + branch)
        .astype(jnp.bfloat16)
        .reshape(row_count, col_count, local_ch)
    )
    grad_flat = cotangent.reshape(pixel_count, local_ch)
    partial = lax.dot_general(
        w_out, grad_flat, (((1,), (1,)), ((), ())), preferred_element_type=jnp.float32
    ).astype(jnp.bfloat16)
    d_two = (
        lax.psum_scatter(partial, "ch", scatter_dimension=0, tiled=True).astype(jnp.float32).T
    )
    grad_two = (d_two * silu_slope(pre_two)).astype(jnp.bfloat16)
    padded_two = group_view(
        row_rims(grad_two.reshape(row_count, col_count, local_mid)), group_width
    )
    d_one = jnp.zeros((row_count, col_count, local_mid // group_width, group_width), jnp.float32)
    for row_tap in range(3):
        for col_tap in range(3):
            window = padded_two[
                2 - row_tap : 2 - row_tap + row_count, 2 - col_tap : 2 - col_tap + col_count
            ]
            d_one = d_one + jnp.einsum(
                "rcgj,igj->rcgi",
                window,
                filters[row_tap, col_tap],
                preferred_element_type=jnp.float32,
            )
    grad_one = (d_one.reshape(pixel_count, local_mid) * silu_slope(pre_one)).astype(jnp.bfloat16)
    grad_view = group_view(grad_two.reshape(row_count, col_count, local_mid), group_width)
    tap_rows = []
    for row_tap in range(3):
        tap_line = []
        for col_tap in range(3):
            window = padded_one[row_tap : row_tap + row_count, col_tap : col_tap + col_count]
            tap_line.append(
                jnp.einsum("rcgi,rcgj->igj", window, grad_view, preferred_element_type=jnp.float32)
            )
        tap_rows.append(jnp.stack(tap_line))
    group_grad = jnp.stack(tap_rows).reshape(3, 3, group_width, local_mid)
    rows = lax.axis_size("row")
    spread = rows * flat_in.size * flat_in.dtype.itemsize <= GATHER_BYTES
    left_in, right_in, left_out, right_out = flat_in, grad_one, mid_full, grad_flat
    if spread:
        left_in, right_in, left_out, right_out = (
            lax.all_gather(v, "row", axis=0, tiled=True)
            for v in (flat_in, grad_one, mid_full, grad_flat)
        )
    in_grad = lax.dot_general(
        left_in, right_in, (((0,), (0,)), ((), ())), preferred_element_type=jnp.float32
    ).astype(jnp.bfloat16)
    out_grad = lax.dot_general(
        left_out, right_out, (((0,), (0,)), ((), ())), preferred_element_type=jnp.float32
    ).astype(jnp.bfloat16)
    if not spread:
        in_grad, out_grad = lax.psum((in_grad, out_grad), "row")
    d_input = (
        lax.psum_scatter(
            lax.dot_general(
                w_in, grad_one, (((1,), (1,)), ((), ())), preferred_element_type=jnp.float32
            ).astype(jnp.bfloat16),
            "ch",
            scatter_dimension=0,
            tiled=True,
        )
        .astype(jnp.float32)
        .T
    )
    grad_input = (
        (grad_flat.astype(jnp.float32) + d_input)
        .astype(jnp.bfloat16)
        .reshape(row_count, col_count, local_ch)
    )
    group_grad = lax.psum(group_grad.astype(jnp.bfloat16), "row")
    return block_out, grad_input, in_grad, group_grad, out_grad


def dot(a, b):
    return jnp.dot(a, b, preferred_element_type=F32)


def dot_nt(a, b):
    return lax.dot_general(a, b, (((1,), (1,)), ((), ())), preferred_element_type=F32)


def dot_tn(a, b):
    return lax.dot_general(a, b, (((0,), (0,)), ((), ())), preferred_element_type=F32)


def moved(values, step):
    count = values.shape[0]
    at = lax.broadcasted_iota(jnp.int32, values.shape, 0)
    edge = 0 if step == 1 else count - 1
    return jnp.where(at == edge, 0.0, pltpu.roll(values, step % count, 0))


class Fabric:
    def __init__(self):
        self.row = lax.axis_index("row")
        self.ch = lax.axis_index("ch")
        self.core = lax.rem(self.ch, 2)
        self.z = self.ch // 2
        self.zs = lax.axis_size("ch") // 2
        x, y = lax.rem(self.row, 2), self.row // 2
        self.row_x = y * 2 + (1 - x)
        self.row_y = (1 - y) * 2 + x
        self.row_d = (1 - y) * 2 + (1 - x)
        self.twin = self.z * 2 + (1 - self.core)
        self.sent = []

    def z_at(self, d):
        return lax.rem(self.z + d, self.zs)

    def ch_at(self, d):
        return self.z_at(d) * 2 + self.core

    def partners(self):
        out = [(self.row, self.ch_at(d)) for d in range(1, self.zs)]
        out += [(r, self.ch) for r in (self.row_x, self.row_y, self.row_d)]
        return out + [(self.row, self.twin)]

    def send(self, src, dst, send_sem, recv_sem, device):
        copy = pltpu.make_async_remote_copy(
            src_ref=src,
            dst_ref=dst,
            send_sem=send_sem,
            recv_sem=recv_sem,
            device_id=device,
            device_id_type=MESH,
        )
        copy.start()
        self.sent.append(copy)

    def arrived(self, dst, sem):
        pltpu.make_async_remote_copy(
            src_ref=dst,
            dst_ref=dst,
            send_sem=sem,
            recv_sem=sem,
            device_id=(self.row, self.twin),
            device_id_type=MESH,
        ).wait_recv()


class Gather:
    def __init__(self, fab, buf, recv, send_z, send_x, send_y, send_t):
        self.fab, self.buf, self.recv = fab, buf, recv
        self.send_z, self.send_x, self.send_y, self.send_t = send_z, send_x, send_y, send_t

    def push(self, k, r, send_sem, device):
        slot = self.buf.at[k, r]
        self.fab.send(slot, slot, send_sem, self.recv.at[k, r], device)

    def to_x(self, k, r, n):
        self.push(k, r, self.send_x.at[n], (self.fab.row_x, self.fab.ch))

    def to_y(self, k, r, n):
        self.push(k, r, self.send_y.at[n], (self.fab.row_y, self.fab.ch))

    def to_twin(self, k, r, n):
        self.push(k, r, self.send_t.at[n], (self.fab.row, self.fab.twin))

    def wait(self, k, r):
        self.fab.arrived(self.buf.at[k, r], self.recv.at[k, r])

    def start(self):
        f = self.fab
        for d in range(1, f.zs):
            self.push(f.ch, f.row, self.send_z.at[d - 1], (f.row, f.ch_at(d)))
        self.to_x(f.ch, f.row, 0)
        self.to_y(f.ch, f.row, 0)
        self.to_twin(f.ch, f.row, 0)

    def land_z(self, d):
        f = self.fab
        self.wait(f.ch_at(d), f.row)
        self.to_twin(f.ch_at(d), f.row, d)

    def spread_z(self, d):
        f = self.fab
        self.to_x(f.ch_at(d), f.row, d)
        self.to_y(f.ch_at(d), f.row, d)

    def pump_xy(self, d):
        f = self.fab
        half = f.zs // 2
        k = f.ch_at(d)
        self.wait(k, f.row_x)
        if d < half:
            self.to_y(k, f.row_x, f.zs + d)
        self.to_twin(k, f.row_x, f.zs + d)
        self.wait(k, f.row_y)
        if d >= half:
            self.to_x(k, f.row_y, f.zs + d - half)
        self.to_twin(k, f.row_y, 2 * f.zs + d)

    def pump_d(self, d):
        f = self.fab
        k = f.ch_at(d)
        self.wait(k, f.row_d)
        self.to_twin(k, f.row_d, 3 * f.zs + d)

    def from_twin(self, d, r):
        f = self.fab
        self.wait(f.z_at(d) * 2 + (1 - f.core), r)


class Scatter:
    def __init__(self, fab, give, got, out, far, acc, give_s, got_s, out_s, far_s):
        self.fab, self.give, self.got, self.out, self.far, self.acc = fab, give, got, out, far, acc
        self.give_s, self.got_s, self.out_s, self.far_s = give_s, got_s, out_s, far_s

    def part(self, lhs, w_ref, k):
        width = lhs.shape[1]
        rows = pl.ds(pl.multiple_of(k * width, width), width)
        return dot_nt(lhs, w_ref[rows, :])

    def start(self, lhs, w_ref):
        f = self.fab
        for d in (1, 2, 3, 0):
            at = f.z_at(d)
            self.give[at] = self.part(lhs, w_ref, at * 2 + (1 - f.core)).astype(BF)
            f.send(
                self.give.at[at],
                self.got.at[at],
                self.give_s.at[d],
                self.got_s.at[at],
                (f.row, f.twin),
            )

    def middle(self, lhs, w_ref):
        f = self.fab
        for d in (1, 2, 3, 0):
            at = f.z_at(d)
            own = self.part(lhs, w_ref, at * 2 + f.core)
            f.arrived(self.got.at[at], self.got_s.at[at])
            own = own + self.got[at].astype(F32)
            if d == 0:
                self.acc[...] = own
            else:
                self.out[at] = own.astype(BF)
                f.send(
                    self.out.at[at],
                    self.far.at[f.z],
                    self.out_s.at[d - 1],
                    self.far_s.at[f.z],
                    (f.row, f.ch_at(d)),
                )

    def finish(self):
        f = self.fab
        for d in (1, 2, 3):
            at = f.z_at(d)
            f.arrived(self.far.at[at], self.far_s.at[at])
        total = self.acc[...]
        for d in (1, 2, 3):
            total = total + self.far[f.z_at(d)].astype(F32)
        return total


def block_kernel(*refs):
    (feat, w_in_hbm, wg, w_out_hbm, cot, out, g_in, gw_in, gw_group, gw_out) = refs[:10]
    (b1, b2, w_in, w_out, pre, act, gt, g1, cots, shifted, wide, stage) = refs[10:22]
    (r1, z1, x1, y1, t1, r2, z2, x2, y2, t2) = refs[22:32]
    s1, s2 = refs[32:41], refs[41:50]
    cot_send, cot_recv, gt_send, gt_recv, halo_send, halo_recv, local = refs[50:57]
    fab = Fabric()
    rows = cots.shape[0]
    pixels, width = feat.shape
    chunk = wide.shape[2]
    gw = wg.shape[1]
    count_k = b1.shape[0]
    chunks = [slice(i * chunk, (i + 1) * chunk) for i in range(width // chunk)]

    load_out = pltpu.make_async_copy(w_out_hbm, w_out, local.at[0])
    load_in = pltpu.make_async_copy(w_in_hbm, w_in, local.at[1])
    load_out.start()
    load_in.start()
    barrier = pltpu.get_barrier_semaphore()
    partners = fab.partners()
    for device in partners:
        pl.semaphore_signal(barrier, inc=1, device_id=device, device_id_type=MESH)
    pl.semaphore_wait(barrier, len(partners))

    gather1 = Gather(fab, b1, r1, z1, x1, y1, t1)
    gather2 = Gather(fab, b2, r2, z2, x2, y2, t2)
    scatter1 = Scatter(fab, *s1)
    scatter2 = Scatter(fab, *s2)
    other_rows = (fab.row_x, fab.row_y, fab.row_d)

    b1[fab.ch, fab.row] = feat[...]
    gather1.start()
    cots[fab.row] = cot[...]
    for n, r in enumerate(other_rows):
        fab.send(
            cots.at[fab.row],
            cots.at[fab.row],
            cot_send.at[n],
            cot_recv.at[fab.row],
            (r, fab.ch),
        )
    load_out.wait()
    scatter1.start(cot[...], w_out)

    blank = jnp.zeros((pixels, width), BF)
    act[0] = blank
    act[rows + 1] = blank
    gt[0] = blank
    gt[rows + 1] = blank
    row_group = lax.broadcasted_iota(jnp.int32, (chunk, chunk), 0) // gw
    col_group = lax.broadcasted_iota(jnp.int32, (chunk, chunk), 1) // gw
    same = row_group == col_group

    def widen(tap, carry):
        for i, part in enumerate(chunks):
            taps = wg[tap, :, part].astype(F32)
            dense = jnp.concatenate([taps] * (chunk // gw), axis=0)
            wide[tap, i] = jnp.where(same, dense, 0.0).astype(BF)
        return carry

    lax.fori_loop(0, 9, widen, 0)

    depths = range(fab.zs)
    load_in.wait()

    def first(r):
        for d in depths:
            gather1.from_twin(d, r)
        pre[r] = jnp.zeros((pixels, width), F32)

        def add(k, carry):
            lines = pl.ds(pl.multiple_of(k * width, width), width)
            pre[r] += dot(b1[k, r], w_in[lines, :])
            return carry

        lax.fori_loop(0, count_k, add, 0)
        value = pre[r]
        act[r + 1] = (value * jax.nn.sigmoid(value)).astype(BF)

    for d in depths[1:]:
        gather1.land_z(d)
    first(fab.row)
    above, below = fab.row > 0, fab.row < rows - 1

    def halo(n, r):
        return pltpu.make_async_remote_copy(
            src_ref=act.at[fab.row + 1],
            dst_ref=act.at[fab.row + 1],
            send_sem=halo_send.at[n],
            recv_sem=halo_recv.at[n],
            device_id=(r, fab.ch),
            device_id_type=MESH,
        )

    def halo_from(n, r):
        return pltpu.make_async_remote_copy(
            src_ref=act.at[r + 1],
            dst_ref=act.at[r + 1],
            send_sem=halo_send.at[n],
            recv_sem=halo_recv.at[n],
            device_id=(r, fab.ch),
            device_id_type=MESH,
        )

    @pl.when(above)
    def _():
        halo(0, fab.row - 1).start()

    @pl.when(below)
    def _():
        halo(1, fab.row + 1).start()

    for d in depths[1:]:
        gather1.spread_z(d)
    scatter1.middle(cot[...], w_out)

    @pl.when(above)
    def _():
        halo(0, fab.row - 1).wait_send()
        halo_from(1, fab.row - 1).wait_recv()

    @pl.when(below)
    def _():
        halo(1, fab.row + 1).wait_send()
        halo_from(0, fab.row + 1).wait_recv()

    taps_of = [[a * 3 + b for a in range(3)] for b in range(3)]
    two = []
    for i, part in enumerate(chunks):
        total = None
        for b in range(3):
            side = None
            for a in range(3):
                term = dot(act[fab.row + a, :, part], wide[taps_of[b][a], i])
                side = term if side is None else side + term
            side = moved(side, 1) if b == 0 else moved(side, -1) if b == 2 else side
            total = side if total is None else total + side
        two.append(total)
    slopes = []
    for i, part in enumerate(chunks):
        b2[fab.ch, fab.row, :, part] = (two[i] * jax.nn.sigmoid(two[i])).astype(BF)
        slopes.append(silu_slope(two[i]))
    gather2.start()
    for d in depths:
        gather1.pump_xy(d)
    first(fab.row_x)
    first(fab.row_y)
    d_two = scatter1.finish()
    for i, part in enumerate(chunks):
        gt[fab.row + 1, :, part] = (d_two[:, part] * slopes[i]).astype(BF)
    for n, r in enumerate(other_rows):
        fab.send(
            gt.at[fab.row + 1],
            gt.at[fab.row + 1],
            gt_send.at[n],
            gt_recv.at[fab.row],
            (r, fab.ch),
        )
    for d in depths:
        gather1.pump_d(d)
    for d in depths[1:]:
        gather2.land_z(d)
        gather2.spread_z(d)
    first(fab.row_d)
    for r in other_rows:
        fab.arrived(gt.at[r + 1], gt_recv.at[r])

    def back(q, carry):
        for i, part in enumerate(chunks):
            total = None
            for b in range(3):
                side = None
                for a in range(3):
                    term = dot_nt(gt[q + 2 - a, :, part], wide[taps_of[b][a], i])
                    side = term if side is None else side + term
                side = moved(side, -1) if b == 0 else moved(side, 1) if b == 2 else side
                total = side if total is None else total + side
            g1[q, :, part] = (total * silu_slope(pre[q, :, part])).astype(BF)
        return carry

    lax.fori_loop(0, rows, back, 0)
    scatter2.start(g1[fab.row], w_in)
    scatter2.middle(g1[fab.row], w_in)

    for d in depths:
        gather2.from_twin(d, fab.row)
    pre[0] = feat[...].astype(F32)

    def last(k, carry):
        lines = pl.ds(pl.multiple_of(k * width, width), width)
        pre[0] += dot(b2[k, fab.row], w_out[lines, :])
        return carry

    lax.fori_loop(0, count_k, last, 0)
    out[...] = pre[0].astype(BF)

    def weight_grad(left, right, result, sems, d):
        def store(slot):
            k = fab.z_at(d) * 2 + slot
            return pltpu.make_async_copy(
                stage.at[slot],
                result.at[pl.ds(pl.multiple_of(k * width, width), width), :],
                sems.at[slot],
            )

        def step(slot, carry):
            lhs = left[fab.z_at(d) * 2 + slot].reshape(rows * pixels, width)
            rhs = right[...].reshape(rows * pixels, width)
            full = dot_tn(lhs, rhs).astype(BF)
            if d > 0:
                store(slot).wait()
            stage[slot] = full
            store(slot).start()
            return carry

        lax.fori_loop(0, 2, step, 0)
        if d == fab.zs - 1:
            for slot in range(2):
                store(slot).wait()

    for d in depths:
        weight_grad(b1, g1, gw_in, local.at[pl.ds(2, 2)], d)
        gather2.pump_xy(d)

    for b in range(3):

        def move(q, carry):
            value = gt[q + 1].astype(F32)
            value = moved(value, -1) if b == 0 else moved(value, 1) if b == 2 else value
            shifted[q] = value.astype(BF)
            return carry

        lax.fori_loop(0, rows, move, 0)

        def tap_grad(a, carry):
            for part in chunks:
                lhs = act[pl.ds(a, rows), :, part].reshape(rows * pixels, chunk)
                full = dot_tn(lhs, shifted[:, :, part].reshape(rows * pixels, chunk))
                full = jnp.where(same, full, 0.0).reshape(chunk // gw, gw, chunk)
                gw_group[a * 3 + b, :, part] = jnp.sum(full, axis=0).astype(BF)
            return carry

        lax.fori_loop(0, 3, tap_grad, 0)

    g_in[...] = (cot[...].astype(F32) + scatter2.finish()).astype(BF)
    for r in other_rows:
        fab.arrived(cots.at[r], cot_recv.at[r])
    for d in depths:
        gather2.pump_d(d)
        for r in other_rows:
            gather2.from_twin(d, r)
        weight_grad(b2, cots, gw_out, local.at[pl.ds(4, 2)], d)
    for copy in fab.sent:
        copy.wait_send()


def body(features, w_in, w_group, w_out, cotangent):
    row_count, pixels, width = features.shape
    rows, lanes = lax.axis_size("row"), lax.axis_size("ch")
    total = rows * lanes * features.size * features.dtype.itemsize
    fits = (rows, lanes, row_count) == (4, 8, 1) and w_in.shape[1] == width == 512
    if not fits or total > GATHER_BYTES:
        return wide_body(features, w_in, w_group, w_out, cotangent)
    zs = lanes // 2
    channels = w_in.shape[0]
    gw = w_group.shape[2]
    dma = pltpu.SemaphoreType.DMA
    vmem = pltpu.VMEM
    gather_sems = [dma((lanes, rows)), dma((zs - 1,)), dma((6,)), dma((6,)), dma((rows * zs,))]
    part = vmem((zs, pixels, width), BF)
    scatter = [part, part, part, part, vmem((pixels, width), F32)]
    scatter += [dma((zs,)), dma((zs,)), dma((zs - 1,)), dma((zs,))]
    scratch = [
        vmem((lanes, rows, pixels, width), BF),
        vmem((lanes, rows, pixels, width), BF),
        vmem((channels, width), BF),
        vmem((channels, width), BF),
        vmem((rows, pixels, width), F32),
        vmem((rows + 2, pixels, width), BF),
        vmem((rows + 2, pixels, width), BF),
        vmem((rows, pixels, width), BF),
        vmem((rows, pixels, width), BF),
        vmem((rows, pixels, width), BF),
        vmem((9, width // 256, 256, 256), BF),
        vmem((2, width, width), BF),
    ]
    scratch += gather_sems * 2 + scatter * 2
    scratch += [dma((3,)), dma((rows,)), dma((3,)), dma((rows,)), dma((2,)), dma((2,)), dma((6,))]
    in_vmem = pl.BlockSpec(memory_space=pltpu.VMEM)
    in_any = pl.BlockSpec(memory_space=pl.ANY)
    flat = jax.ShapeDtypeStruct((pixels, width), BF)
    weight = jax.ShapeDtypeStruct((channels, width), BF)
    out, g_in, gw_in, gw_group, gw_out = pl.pallas_call(
        block_kernel,
        out_shape=[flat, flat, weight, jax.ShapeDtypeStruct((9, gw, width), BF), weight],
        in_specs=[in_vmem, in_any, in_vmem, in_any, in_vmem],
        out_specs=[in_vmem, in_vmem, in_any, in_vmem, in_any],
        scratch_shapes=scratch,
        compiler_params=pltpu.CompilerParams(
            collective_id=0, has_side_effects=True, vmem_limit_bytes=60 * 1024 * 1024
        ),
    )(
        features.reshape(pixels, width),
        w_in,
        w_group.reshape(9, gw, width),
        w_out,
        cotangent.reshape(pixels, width),
    )
    return (
        out.reshape(features.shape),
        g_in.reshape(features.shape),
        gw_in,
        gw_group.reshape(w_group.shape),
        gw_out,
    )


def solution(mesh):
    placed = (
        P("row", None, "ch"),
        P(None, "ch"),
        P(None, None, None, "ch"),
        P(None, "ch"),
        P("row", None, "ch"),
    )
    return jax.shard_map(
        body,
        mesh=mesh,
        in_specs=placed,
        out_specs=(
            P("row", None, "ch"),
            P("row", None, "ch"),
            P(None, "ch"),
            P(None, None, None, "ch"),
            P(None, "ch"),
        ),
        check_vma=False,
    )
```

```python
import jax
import jax.numpy as jnp
from jax import lax
from jax.experimental import pallas as pl
from jax.experimental.pallas import tpu as pltpu
from jax.sharding import PartitionSpec as P


GATHER_BYTES = 8 * 1024 * 1024
MESH = pl.DeviceIdType.MESH
BF = jnp.bfloat16
F32 = jnp.float32


def padded_2(cells, sides, width):
    for axis, dim in sides:
        count = lax.axis_size(axis)
        ends = count - 1
        head = lax.slice_in_dim(cells, 0, width, axis=dim)
        tail = lax.slice_in_dim(cells, cells.shape[dim] - width, cells.shape[dim], axis=dim)
        cells = jnp.concatenate(
            [
                lax.ppermute(tail, axis, [(i, (i + 1) % count) for i in range(ends)]),
                cells,
                lax.ppermute(head, axis, [((i + 1) % count, i) for i in range(ends)]),
            ],
            axis=dim,
        )
    return cells


def silu_slope(values):
    sigma = jax.nn.sigmoid(values)
    return sigma * (1.0 + values * (1.0 - sigma))


def full_channels(local):
    return lax.all_gather(local, "ch", axis=2, tiled=True)


def row_rims(local):
    padded = padded_2(local, (("row", 0),), 1)
    return jnp.pad(padded, ((0, 0), (1, 1), (0, 0)))


def group_view(local, group_width):
    return local.reshape(local.shape[0], local.shape[1], local.shape[2] // group_width, group_width)


def wide_body(features, w_in, w_group, w_out, cotangent):
    row_count, col_count, local_ch = features.shape
    group_width = w_group.shape[2]
    local_mid = w_in.shape[1]
    pixel_count = row_count * col_count
    gathered = full_channels(features)
    flat_in = gathered.reshape(pixel_count, -1)
    pre_one = jnp.dot(flat_in, w_in, preferred_element_type=jnp.float32)
    act_one = jax.nn.silu(pre_one).astype(jnp.bfloat16).reshape(row_count, col_count, local_mid)
    padded_one = group_view(row_rims(act_one), group_width)
    filters = w_group.reshape(3, 3, group_width, local_mid // group_width, group_width)
    pre_two = jnp.zeros((row_count, col_count, local_mid // group_width, group_width), jnp.float32)
    for row_tap in range(3):
        for col_tap in range(3):
            window = padded_one[row_tap : row_tap + row_count, col_tap : col_tap + col_count]
            pre_two = pre_two + jnp.einsum(
                "rcgi,igj->rcgj",
                window,
                filters[row_tap, col_tap],
                preferred_element_type=jnp.float32,
            )
    pre_two = pre_two.reshape(pixel_count, local_mid)
    act_two = jax.nn.silu(pre_two).astype(jnp.bfloat16)
    mid_full = full_channels(act_two.reshape(row_count, col_count, local_mid)).reshape(
        pixel_count, -1
    )
    branch = jnp.dot(mid_full, w_out, preferred_element_type=jnp.float32)
    flat_local = features.reshape(pixel_count, local_ch)
    block_out = (
        (flat_local.astype(jnp.float32) + branch)
        .astype(jnp.bfloat16)
        .reshape(row_count, col_count, local_ch)
    )
    grad_flat = cotangent.reshape(pixel_count, local_ch)
    partial = lax.dot_general(
        w_out, grad_flat, (((1,), (1,)), ((), ())), preferred_element_type=jnp.float32
    ).astype(jnp.bfloat16)
    d_two = (
        lax.psum_scatter(partial, "ch", scatter_dimension=0, tiled=True).astype(jnp.float32).T
    )
    grad_two = (d_two * silu_slope(pre_two)).astype(jnp.bfloat16)
    padded_two = group_view(
        row_rims(grad_two.reshape(row_count, col_count, local_mid)), group_width
    )
    d_one = jnp.zeros((row_count, col_count, local_mid // group_width, group_width), jnp.float32)
    for row_tap in range(3):
        for col_tap in range(3):
            window = padded_two[
                2 - row_tap : 2 - row_tap + row_count, 2 - col_tap : 2 - col_tap + col_count
            ]
            d_one = d_one + jnp.einsum(
                "rcgj,igj->rcgi",
                window,
                filters[row_tap, col_tap],
                preferred_element_type=jnp.float32,
            )
    grad_one = (d_one.reshape(pixel_count, local_mid) * silu_slope(pre_one)).astype(jnp.bfloat16)
    grad_view = group_view(grad_two.reshape(row_count, col_count, local_mid), group_width)
    tap_rows = []
    for row_tap in range(3):
        tap_line = []
        for col_tap in range(3):
            window = padded_one[row_tap : row_tap + row_count, col_tap : col_tap + col_count]
            tap_line.append(
                jnp.einsum("rcgi,rcgj->igj", window, grad_view, preferred_element_type=jnp.float32)
            )
        tap_rows.append(jnp.stack(tap_line))
    group_grad = jnp.stack(tap_rows).reshape(3, 3, group_width, local_mid)
    rows = lax.axis_size("row")
    spread = rows * flat_in.size * flat_in.dtype.itemsize <= GATHER_BYTES
    left_in, right_in, left_out, right_out = flat_in, grad_one, mid_full, grad_flat
    if spread:
        left_in, right_in, left_out, right_out = (
            lax.all_gather(v, "row", axis=0, tiled=True)
            for v in (flat_in, grad_one, mid_full, grad_flat)
        )
    in_grad = lax.dot_general(
        left_in, right_in, (((0,), (0,)), ((), ())), preferred_element_type=jnp.float32
    ).astype(jnp.bfloat16)
    out_grad = lax.dot_general(
        left_out, right_out, (((0,), (0,)), ((), ())), preferred_element_type=jnp.float32
    ).astype(jnp.bfloat16)
    if not spread:
        in_grad, out_grad = lax.psum((in_grad, out_grad), "row")
    d_input = (
        lax.psum_scatter(
            lax.dot_general(
                w_in, grad_one, (((1,), (1,)), ((), ())), preferred_element_type=jnp.float32
            ).astype(jnp.bfloat16),
            "ch",
            scatter_dimension=0,
            tiled=True,
        )
        .astype(jnp.float32)
        .T
    )
    grad_input = (
        (grad_flat.astype(jnp.float32) + d_input)
        .astype(jnp.bfloat16)
        .reshape(row_count, col_count, local_ch)
    )
    group_grad = lax.psum(group_grad.astype(jnp.bfloat16), "row")
    return block_out, grad_input, in_grad, group_grad, out_grad


def dot(a, b):
    return jnp.dot(a, b, preferred_element_type=F32)


def dot_nt(a, b):
    return lax.dot_general(a, b, (((1,), (1,)), ((), ())), preferred_element_type=F32)


def dot_tn(a, b):
    return lax.dot_general(a, b, (((0,), (0,)), ((), ())), preferred_element_type=F32)


def moved(values, step):
    count = values.shape[0]
    at = lax.broadcasted_iota(jnp.int32, values.shape, 0)
    edge = 0 if step == 1 else count - 1
    return jnp.where(at == edge, 0.0, pltpu.roll(values, step % count, 0))


class Fabric:
    def __init__(self):
        self.row = lax.axis_index("row")
        self.ch = lax.axis_index("ch")
        self.core = lax.rem(self.ch, 2)
        self.z = self.ch // 2
        self.zs = lax.axis_size("ch") // 2
        x, y = lax.rem(self.row, 2), self.row // 2
        self.row_x = y * 2 + (1 - x)
        self.row_y = (1 - y) * 2 + x
        self.row_d = (1 - y) * 2 + (1 - x)
        self.twin = self.z * 2 + (1 - self.core)
        self.sent = []
        self.held = []

    def z_at(self, d):
        return lax.rem(self.z + d, self.zs)

    def ch_at(self, d):
        return self.z_at(d) * 2 + self.core

    def partners(self):
        out = [(self.row, self.ch_at(d)) for d in range(1, self.zs)]
        out += [(r, self.ch) for r in (self.row_x, self.row_y, self.row_d)]
        return out + [(self.row, self.twin)]

    def send(self, src, dst, send_sem, recv_sem, device):
        copy = pltpu.make_async_remote_copy(
            src_ref=src,
            dst_ref=dst,
            send_sem=send_sem,
            recv_sem=recv_sem,
            device_id=device,
            device_id_type=MESH,
        )
        copy.start()
        self.sent.append(copy)

    def arrived(self, dst, sem):
        pltpu.make_async_remote_copy(
            src_ref=dst,
            dst_ref=dst,
            send_sem=sem,
            recv_sem=sem,
            device_id=(self.row, self.twin),
            device_id_type=MESH,
        ).wait_recv()


class Gather:
    def __init__(self, fab, buf, recv, send_z, send_x, send_y, send_t):
        self.fab, self.buf, self.recv = fab, buf, recv
        self.send_z, self.send_x, self.send_y, self.send_t = send_z, send_x, send_y, send_t

    def push(self, k, r, send_sem, device):
        slot = self.buf.at[k, r]
        self.fab.send(slot, slot, send_sem, self.recv.at[k, r], device)

    def to_x(self, k, r, n):
        self.push(k, r, self.send_x.at[n], (self.fab.row_x, self.fab.ch))

    def to_y(self, k, r, n):
        self.push(k, r, self.send_y.at[n], (self.fab.row_y, self.fab.ch))

    def to_twin(self, k, r, n):
        self.push(k, r, self.send_t.at[n], (self.fab.row, self.fab.twin))

    def wait(self, k, r):
        self.fab.arrived(self.buf.at[k, r], self.recv.at[k, r])

    def start(self):
        f = self.fab
        self.relay(0, 1)
        self.relay(0, -1)
        self.to_x(f.ch, f.row, 0)
        self.to_y(f.ch, f.row, 0)
        self.to_twin(f.ch, f.row, 0)

    def relay(self, d, way):
        f = self.fab
        k = f.ch_at(d)
        slot = self.buf.at[k, f.row]
        sem = self.send_z.at[f.zs if d == 0 and way == 1 else d]

        def copy():
            return pltpu.make_async_remote_copy(
                src_ref=slot,
                dst_ref=slot,
                send_sem=sem,
                recv_sem=self.recv.at[k, f.row],
                device_id=(f.row, f.ch + 2 * way),
                device_id_type=MESH,
            )

        above = f.z + d < f.zs
        came = True if d == 0 else above if way == -1 else jnp.logical_not(above)
        more = f.z > 0 if way == -1 else f.z < f.zs - 1
        go = more if d == 0 else jnp.logical_and(came, more)

        @pl.when(go)
        def _():
            copy().start()

        f.held.append((go, copy))

    def land_z(self, step):
        f = self.fab
        for d, way in ((step, -1), (f.zs - step, 1)):
            here = f.z + d < f.zs if way == -1 else f.z + d >= f.zs

            @pl.when(here)
            def _():
                self.wait(f.ch_at(d), f.row)

            self.relay(d, way)

            @pl.when(here)
            def _():
                self.twin_copy(d).start()

    def twin_copy(self, d):
        f = self.fab
        slot = self.buf.at[f.ch_at(d), f.row]
        return pltpu.make_async_remote_copy(
            src_ref=slot,
            dst_ref=slot,
            send_sem=self.send_t.at[d],
            recv_sem=self.recv.at[f.ch_at(d), f.row],
            device_id=(f.row, f.twin),
            device_id_type=MESH,
        )

    def landed_z(self):
        for d in range(1, self.fab.zs):
            self.fab.sent.append(self.twin_copy(d))

    def spread_z(self, d):
        f = self.fab
        self.to_x(f.ch_at(d), f.row, d)
        self.to_y(f.ch_at(d), f.row, d)

    def pump_xy(self, d):
        f = self.fab
        half = f.zs // 2
        k = f.ch_at(d)
        self.wait(k, f.row_x)
        if d < half:
            self.to_y(k, f.row_x, f.zs + d)
        self.to_twin(k, f.row_x, f.zs + d)
        self.wait(k, f.row_y)
        if d >= half:
            self.to_x(k, f.row_y, f.zs + d - half)
        self.to_twin(k, f.row_y, 2 * f.zs + d)

    def pump_d(self, d):
        f = self.fab
        k = f.ch_at(d)
        self.wait(k, f.row_d)
        self.to_twin(k, f.row_d, 3 * f.zs + d)

    def from_twin(self, d, r):
        f = self.fab
        self.wait(f.z_at(d) * 2 + (1 - f.core), r)


class Scatter:
    def __init__(self, fab, give, got, out, far, acc, give_s, got_s, out_s, far_s):
        self.fab, self.give, self.got, self.out, self.far, self.acc = fab, give, got, out, far, acc
        self.give_s, self.got_s, self.out_s, self.far_s = give_s, got_s, out_s, far_s

    def part(self, lhs, w_ref, k):
        width = lhs.shape[1]
        rows = pl.ds(pl.multiple_of(k * width, width), width)
        return dot_nt(lhs, w_ref[rows, :])

    def start(self, lhs, w_ref):
        f = self.fab
        for d in (1, 2, 3, 0):
            at = f.z_at(d)
            self.give[at] = self.part(lhs, w_ref, at * 2 + (1 - f.core)).astype(BF)
            f.send(
                self.give.at[at],
                self.got.at[at],
                self.give_s.at[d],
                self.got_s.at[at],
                (f.row, f.twin),
            )

    def middle(self, lhs, w_ref):
        f = self.fab
        for d in (1, 2, 3, 0):
            at = f.z_at(d)
            own = self.part(lhs, w_ref, at * 2 + f.core)
            f.arrived(self.got.at[at], self.got_s.at[at])
            own = own + self.got[at].astype(F32)
            if d == 0:
                self.acc[...] = own
            else:
                self.out[at] = own.astype(BF)
                f.send(
                    self.out.at[at],
                    self.far.at[f.z],
                    self.out_s.at[d - 1],
                    self.far_s.at[f.z],
                    (f.row, f.ch_at(d)),
                )

    def finish(self):
        f = self.fab
        for d in (1, 2, 3):
            at = f.z_at(d)
            f.arrived(self.far.at[at], self.far_s.at[at])
        total = self.acc[...]
        for d in (1, 2, 3):
            total = total + self.far[f.z_at(d)].astype(F32)
        return total


def block_kernel(*refs):
    (feat, w_in_hbm, wg, w_out_hbm, cot, out, g_in, gw_in, gw_group, gw_out) = refs[:10]
    (b1, b2, w_in, w_out, pre, act, gt, g1, cots, shifted, wide, stage) = refs[10:22]
    (r1, z1, x1, y1, t1, r2, z2, x2, y2, t2) = refs[22:32]
    s1, s2 = refs[32:41], refs[41:50]
    cot_send, cot_recv, gt_send, gt_recv, halo_send, halo_recv, local = refs[50:57]
    fab = Fabric()
    rows = cots.shape[0]
    pixels, width = feat.shape
    chunk = wide.shape[2]
    gw = wg.shape[1]
    count_k = b1.shape[0]
    chunks = [slice(i * chunk, (i + 1) * chunk) for i in range(width // chunk)]

    load_out = pltpu.make_async_copy(w_out_hbm, w_out, local.at[0])
    load_in = pltpu.make_async_copy(w_in_hbm, w_in, local.at[1])
    load_out.start()
    load_in.start()
    barrier = pltpu.get_barrier_semaphore()
    partners = fab.partners()
    for device in partners:
        pl.semaphore_signal(barrier, inc=1, device_id=device, device_id_type=MESH)
    pl.semaphore_wait(barrier, len(partners))

    gather1 = Gather(fab, b1, r1, z1, x1, y1, t1)
    gather2 = Gather(fab, b2, r2, z2, x2, y2, t2)
    scatter1 = Scatter(fab, *s1)
    scatter2 = Scatter(fab, *s2)
    other_rows = (fab.row_x, fab.row_y, fab.row_d)

    b1[fab.ch, fab.row] = feat[...]
    gather1.start()
    cots[fab.row] = cot[...]
    for n, r in enumerate(other_rows):
        fab.send(
            cots.at[fab.row],
            cots.at[fab.row],
            cot_send.at[n],
            cot_recv.at[fab.row],
            (r, fab.ch),
        )
    load_out.wait()
    scatter1.start(cot[...], w_out)

    blank = jnp.zeros((pixels, width), BF)
    act[0] = blank
    act[rows + 1] = blank
    gt[0] = blank
    gt[rows + 1] = blank
    row_group = lax.broadcasted_iota(jnp.int32, (chunk, chunk), 0) // gw
    col_group = lax.broadcasted_iota(jnp.int32, (chunk, chunk), 1) // gw
    same = row_group == col_group

    def widen(tap, carry):
        for i, part in enumerate(chunks):
            taps = wg[tap, :, part].astype(F32)
            dense = jnp.concatenate([taps] * (chunk // gw), axis=0)
            wide[tap, i] = jnp.where(same, dense, 0.0).astype(BF)
        return carry

    lax.fori_loop(0, 9, widen, 0)

    depths = range(fab.zs)
    load_in.wait()

    def first(r):
        for d in depths:
            gather1.from_twin(d, r)
        pre[r] = jnp.zeros((pixels, width), F32)

        def add(k, carry):
            lines = pl.ds(pl.multiple_of(k * width, width), width)
            pre[r] += dot(b1[k, r], w_in[lines, :])
            return carry

        lax.fori_loop(0, count_k, add, 0)
        value = pre[r]
        act[r + 1] = (value * jax.nn.sigmoid(value)).astype(BF)

    for d in depths[1:]:
        gather1.land_z(d)
    gather1.landed_z()
    first(fab.row)
    above, below = fab.row > 0, fab.row < rows - 1

    def halo(n, r):
        return pltpu.make_async_remote_copy(
            src_ref=act.at[fab.row + 1],
            dst_ref=act.at[fab.row + 1],
            send_sem=halo_send.at[n],
            recv_sem=halo_recv.at[n],
            device_id=(r, fab.ch),
            device_id_type=MESH,
        )

    def halo_from(n, r):
        return pltpu.make_async_remote_copy(
            src_ref=act.at[r + 1],
            dst_ref=act.at[r + 1],
            send_sem=halo_send.at[n],
            recv_sem=halo_recv.at[n],
            device_id=(r, fab.ch),
            device_id_type=MESH,
        )

    @pl.when(above)
    def _():
        halo(0, fab.row - 1).start()

    @pl.when(below)
    def _():
        halo(1, fab.row + 1).start()

    for d in depths[1:]:
        gather1.spread_z(d)
    scatter1.middle(cot[...], w_out)

    @pl.when(above)
    def _():
        halo(0, fab.row - 1).wait_send()
        halo_from(1, fab.row - 1).wait_recv()

    @pl.when(below)
    def _():
        halo(1, fab.row + 1).wait_send()
        halo_from(0, fab.row + 1).wait_recv()

    taps_of = [[a * 3 + b for a in range(3)] for b in range(3)]
    two = []
    for i, part in enumerate(chunks):
        total = None
        for b in range(3):
            side = None
            for a in range(3):
                term = dot(act[fab.row + a, :, part], wide[taps_of[b][a], i])
                side = term if side is None else side + term
            side = moved(side, 1) if b == 0 else moved(side, -1) if b == 2 else side
            total = side if total is None else total + side
        two.append(total)
    slopes = []
    for i, part in enumerate(chunks):
        b2[fab.ch, fab.row, :, part] = (two[i] * jax.nn.sigmoid(two[i])).astype(BF)
        slopes.append(silu_slope(two[i]))
    gather2.start()
    gather1.pump_xy(0)
    gather1.pump_xy(1)
    gather2.land_z(1)
    gather1.pump_xy(2)
    gather2.land_z(2)
    gather1.pump_xy(3)
    d_two = scatter1.finish()
    for i, part in enumerate(chunks):
        gt[fab.row + 1, :, part] = (d_two[:, part] * slopes[i]).astype(BF)
    for n, r in enumerate(other_rows):
        fab.send(
            gt.at[fab.row + 1],
            gt.at[fab.row + 1],
            gt_send.at[n],
            gt_recv.at[fab.row],
            (r, fab.ch),
        )
    gather2.land_z(3)
    gather2.landed_z()
    for d in depths[1:]:
        gather2.spread_z(d)
    for d in depths:
        gather1.pump_d(d)
    first(fab.row_x)
    first(fab.row_y)
    first(fab.row_d)
    for r in other_rows:
        fab.arrived(gt.at[r + 1], gt_recv.at[r])

    def back(q, carry):
        for i, part in enumerate(chunks):
            total = None
            for b in range(3):
                side = None
                for a in range(3):
                    term = dot_nt(gt[q + 2 - a, :, part], wide[taps_of[b][a], i])
                    side = term if side is None else side + term
                side = moved(side, -1) if b == 0 else moved(side, 1) if b == 2 else side
                total = side if total is None else total + side
            g1[q, :, part] = (total * silu_slope(pre[q, :, part])).astype(BF)
        return carry

    lax.fori_loop(0, rows, back, 0)
    scatter2.start(g1[fab.row], w_in)
    scatter2.middle(g1[fab.row], w_in)

    for d in depths:
        gather2.from_twin(d, fab.row)
    pre[0] = feat[...].astype(F32)

    def last(k, carry):
        lines = pl.ds(pl.multiple_of(k * width, width), width)
        pre[0] += dot(b2[k, fab.row], w_out[lines, :])
        return carry

    lax.fori_loop(0, count_k, last, 0)
    out[...] = pre[0].astype(BF)

    def weight_grad(left, right, result, sems, d):
        def store(slot):
            k = fab.z_at(d) * 2 + slot
            return pltpu.make_async_copy(
                stage.at[slot],
                result.at[pl.ds(pl.multiple_of(k * width, width), width), :],
                sems.at[slot],
            )

        def step(slot, carry):
            lhs = left[fab.z_at(d) * 2 + slot].reshape(rows * pixels, width)
            rhs = right[...].reshape(rows * pixels, width)
            full = dot_tn(lhs, rhs).astype(BF)
            if d > 0:
                store(slot).wait()
            stage[slot] = full
            store(slot).start()
            return carry

        lax.fori_loop(0, 2, step, 0)
        if d == fab.zs - 1:
            for slot in range(2):
                store(slot).wait()

    for d in depths:
        weight_grad(b1, g1, gw_in, local.at[pl.ds(2, 2)], d)
        gather2.pump_xy(d)

    for b in range(3):

        def move(q, carry):
            value = gt[q + 1].astype(F32)
            value = moved(value, -1) if b == 0 else moved(value, 1) if b == 2 else value
            shifted[q] = value.astype(BF)
            return carry

        lax.fori_loop(0, rows, move, 0)

        def tap_grad(a, carry):
            for part in chunks:
                lhs = act[pl.ds(a, rows), :, part].reshape(rows * pixels, chunk)
                full = dot_tn(lhs, shifted[:, :, part].reshape(rows * pixels, chunk))
                full = jnp.where(same, full, 0.0).reshape(chunk // gw, gw, chunk)
                gw_group[a * 3 + b, :, part] = jnp.sum(full, axis=0).astype(BF)
            return carry

        lax.fori_loop(0, 3, tap_grad, 0)

    g_in[...] = (cot[...].astype(F32) + scatter2.finish()).astype(BF)
    for r in other_rows:
        fab.arrived(cots.at[r], cot_recv.at[r])
    for d in depths:
        gather2.pump_d(d)
        for r in other_rows:
            gather2.from_twin(d, r)
        weight_grad(b2, cots, gw_out, local.at[pl.ds(4, 2)], d)
    for copy in fab.sent:
        copy.wait_send()
    for go, copy in fab.held:

        @pl.when(go)
        def _():
            copy().wait_send()


def hand_over(*refs):
    count = len(refs) // 2
    sems = refs[-1]
    copies = []
    for n, (src, dst) in enumerate(zip(refs[:count], refs[count : 2 * count])):
        parts = 4 if src.shape[0] % 1024 == 0 else 1
        size = src.shape[0] // parts
        for p in range(parts):
            rows = pl.ds(p * size, size)
            copies.append(pltpu.make_async_copy(src.at[rows], dst.at[rows], sems.at[n, p]))
    for copy in copies:
        copy.start()
    for copy in copies:
        copy.wait()


def body(features, w_in, w_group, w_out, cotangent):
    row_count, pixels, width = features.shape
    rows, lanes = lax.axis_size("row"), lax.axis_size("ch")
    total = rows * lanes * features.size * features.dtype.itemsize
    fits = (rows, lanes, row_count) == (4, 8, 1) and w_in.shape[1] == width == 512
    if not fits or total > GATHER_BYTES:
        return wide_body(features, w_in, w_group, w_out, cotangent)
    zs = lanes // 2
    channels = w_in.shape[0]
    gw = w_group.shape[2]
    dma = pltpu.SemaphoreType.DMA
    vmem = pltpu.VMEM
    gather_sems = [dma((lanes, rows)), dma((zs + 1,)), dma((6,)), dma((6,)), dma((rows * zs,))]
    part = vmem((zs, pixels, width), BF)
    scatter = [part, part, part, part, vmem((pixels, width), F32)]
    scatter += [dma((zs,)), dma((zs,)), dma((zs - 1,)), dma((zs,))]
    scratch = [
        vmem((lanes, rows, pixels, width), BF),
        vmem((lanes, rows, pixels, width), BF),
        vmem((channels, width), BF),
        vmem((channels, width), BF),
        vmem((rows, pixels, width), F32),
        vmem((rows + 2, pixels, width), BF),
        vmem((rows + 2, pixels, width), BF),
        vmem((rows, pixels, width), BF),
        vmem((rows, pixels, width), BF),
        vmem((rows, pixels, width), BF),
        vmem((9, width // 256, 256, 256), BF),
        vmem((2, width, width), BF),
    ]
    scratch += gather_sems * 2 + scatter * 2
    scratch += [dma((3,)), dma((rows,)), dma((3,)), dma((rows,)), dma((2,)), dma((2,)), dma((6,))]
    in_vmem = pl.BlockSpec(memory_space=pltpu.VMEM)
    in_any = pl.BlockSpec(memory_space=pl.ANY)
    flat = jax.ShapeDtypeStruct((pixels, width), BF)
    weight = jax.ShapeDtypeStruct((channels, width), BF)
    results = pl.pallas_call(
        block_kernel,
        out_shape=[flat, flat, weight, jax.ShapeDtypeStruct((9, gw, width), BF), weight],
        in_specs=[in_vmem, in_any, in_vmem, in_any, in_vmem],
        out_specs=[in_vmem, in_vmem, in_any, in_vmem, in_any],
        scratch_shapes=scratch,
        compiler_params=pltpu.CompilerParams(
            collective_id=0, has_side_effects=True, vmem_limit_bytes=60 * 1024 * 1024
        ),
    )(
        features.reshape(pixels, width),
        w_in,
        w_group.reshape(9, gw, width),
        w_out,
        cotangent.reshape(pixels, width),
    )
    out, g_in, gw_in, gw_group, gw_out = pl.pallas_call(
        hand_over,
        out_shape=[jax.ShapeDtypeStruct(v.shape, v.dtype) for v in results],
        in_specs=[in_any] * 5,
        out_specs=[in_any] * 5,
        scratch_shapes=[dma((5, 4))],
        compiler_params=pltpu.CompilerParams(vmem_limit_bytes=60 * 1024 * 1024),
    )(*results)
    return (
        out.reshape(features.shape),
        g_in.reshape(features.shape),
        gw_in,
        gw_group.reshape(w_group.shape),
        gw_out,
    )


def solution(mesh):
    placed = (
        P("row", None, "ch"),
        P(None, "ch"),
        P(None, None, None, "ch"),
        P(None, "ch"),
        P("row", None, "ch"),
    )
    return jax.shard_map(
        body,
        mesh=mesh,
        in_specs=placed,
        out_specs=(
            P("row", None, "ch"),
            P("row", None, "ch"),
            P(None, "ch"),
            P(None, None, None, "ch"),
            P(None, "ch"),
        ),
        check_vma=False,
    )
```

```python
import jax
import jax.numpy as jnp
from jax import lax
from jax.experimental import pallas as pl
from jax.experimental.pallas import tpu as pltpu
from jax.sharding import PartitionSpec as P


GATHER_BYTES = 8 * 1024 * 1024
MESH = pl.DeviceIdType.MESH
BF = jnp.bfloat16
F32 = jnp.float32


def padded_2(cells, sides, width):
    for axis, dim in sides:
        count = lax.axis_size(axis)
        ends = count - 1
        head = lax.slice_in_dim(cells, 0, width, axis=dim)
        tail = lax.slice_in_dim(cells, cells.shape[dim] - width, cells.shape[dim], axis=dim)
        cells = jnp.concatenate(
            [
                lax.ppermute(tail, axis, [(i, (i + 1) % count) for i in range(ends)]),
                cells,
                lax.ppermute(head, axis, [((i + 1) % count, i) for i in range(ends)]),
            ],
            axis=dim,
        )
    return cells


def silu_slope(values):
    sigma = jax.nn.sigmoid(values)
    return sigma * (1.0 + values * (1.0 - sigma))


def full_channels(local):
    return lax.all_gather(local, "ch", axis=2, tiled=True)


def row_rims(local):
    padded = padded_2(local, (("row", 0),), 1)
    return jnp.pad(padded, ((0, 0), (1, 1), (0, 0)))


def group_view(local, group_width):
    return local.reshape(local.shape[0], local.shape[1], local.shape[2] // group_width, group_width)


def wide_body(features, w_in, w_group, w_out, cotangent):
    row_count, col_count, local_ch = features.shape
    group_width = w_group.shape[2]
    local_mid = w_in.shape[1]
    pixel_count = row_count * col_count
    gathered = full_channels(features)
    flat_in = gathered.reshape(pixel_count, -1)
    pre_one = jnp.dot(flat_in, w_in, preferred_element_type=jnp.float32)
    act_one = jax.nn.silu(pre_one).astype(jnp.bfloat16).reshape(row_count, col_count, local_mid)
    padded_one = group_view(row_rims(act_one), group_width)
    filters = w_group.reshape(3, 3, group_width, local_mid // group_width, group_width)
    pre_two = jnp.zeros((row_count, col_count, local_mid // group_width, group_width), jnp.float32)
    for row_tap in range(3):
        for col_tap in range(3):
            window = padded_one[row_tap : row_tap + row_count, col_tap : col_tap + col_count]
            pre_two = pre_two + jnp.einsum(
                "rcgi,igj->rcgj",
                window,
                filters[row_tap, col_tap],
                preferred_element_type=jnp.float32,
            )
    pre_two = pre_two.reshape(pixel_count, local_mid)
    act_two = jax.nn.silu(pre_two).astype(jnp.bfloat16)
    mid_full = full_channels(act_two.reshape(row_count, col_count, local_mid)).reshape(
        pixel_count, -1
    )
    branch = jnp.dot(mid_full, w_out, preferred_element_type=jnp.float32)
    flat_local = features.reshape(pixel_count, local_ch)
    block_out = (
        (flat_local.astype(jnp.float32) + branch)
        .astype(jnp.bfloat16)
        .reshape(row_count, col_count, local_ch)
    )
    grad_flat = cotangent.reshape(pixel_count, local_ch)
    partial = lax.dot_general(
        w_out, grad_flat, (((1,), (1,)), ((), ())), preferred_element_type=jnp.float32
    ).astype(jnp.bfloat16)
    d_two = (
        lax.psum_scatter(partial, "ch", scatter_dimension=0, tiled=True).astype(jnp.float32).T
    )
    grad_two = (d_two * silu_slope(pre_two)).astype(jnp.bfloat16)
    padded_two = group_view(
        row_rims(grad_two.reshape(row_count, col_count, local_mid)), group_width
    )
    d_one = jnp.zeros((row_count, col_count, local_mid // group_width, group_width), jnp.float32)
    for row_tap in range(3):
        for col_tap in range(3):
            window = padded_two[
                2 - row_tap : 2 - row_tap + row_count, 2 - col_tap : 2 - col_tap + col_count
            ]
            d_one = d_one + jnp.einsum(
                "rcgj,igj->rcgi",
                window,
                filters[row_tap, col_tap],
                preferred_element_type=jnp.float32,
            )
    grad_one = (d_one.reshape(pixel_count, local_mid) * silu_slope(pre_one)).astype(jnp.bfloat16)
    grad_view = group_view(grad_two.reshape(row_count, col_count, local_mid), group_width)
    tap_rows = []
    for row_tap in range(3):
        tap_line = []
        for col_tap in range(3):
            window = padded_one[row_tap : row_tap + row_count, col_tap : col_tap + col_count]
            tap_line.append(
                jnp.einsum("rcgi,rcgj->igj", window, grad_view, preferred_element_type=jnp.float32)
            )
        tap_rows.append(jnp.stack(tap_line))
    group_grad = jnp.stack(tap_rows).reshape(3, 3, group_width, local_mid)
    rows = lax.axis_size("row")
    spread = rows * flat_in.size * flat_in.dtype.itemsize <= GATHER_BYTES
    left_in, right_in, left_out, right_out = flat_in, grad_one, mid_full, grad_flat
    if spread:
        left_in, right_in, left_out, right_out = (
            lax.all_gather(v, "row", axis=0, tiled=True)
            for v in (flat_in, grad_one, mid_full, grad_flat)
        )
    in_grad = lax.dot_general(
        left_in, right_in, (((0,), (0,)), ((), ())), preferred_element_type=jnp.float32
    ).astype(jnp.bfloat16)
    out_grad = lax.dot_general(
        left_out, right_out, (((0,), (0,)), ((), ())), preferred_element_type=jnp.float32
    ).astype(jnp.bfloat16)
    if not spread:
        in_grad, out_grad = lax.psum((in_grad, out_grad), "row")
    d_input = (
        lax.psum_scatter(
            lax.dot_general(
                w_in, grad_one, (((1,), (1,)), ((), ())), preferred_element_type=jnp.float32
            ).astype(jnp.bfloat16),
            "ch",
            scatter_dimension=0,
            tiled=True,
        )
        .astype(jnp.float32)
        .T
    )
    grad_input = (
        (grad_flat.astype(jnp.float32) + d_input)
        .astype(jnp.bfloat16)
        .reshape(row_count, col_count, local_ch)
    )
    group_grad = lax.psum(group_grad.astype(jnp.bfloat16), "row")
    return block_out, grad_input, in_grad, group_grad, out_grad


def dot(a, b):
    return jnp.dot(a, b, preferred_element_type=F32)


def dot_nt(a, b):
    return lax.dot_general(a, b, (((1,), (1,)), ((), ())), preferred_element_type=F32)


def dot_tn(a, b):
    return lax.dot_general(a, b, (((0,), (0,)), ((), ())), preferred_element_type=F32)


def moved(values, step):
    count = values.shape[0]
    at = lax.broadcasted_iota(jnp.int32, values.shape, 0)
    edge = 0 if step == 1 else count - 1
    return jnp.where(at == edge, 0.0, pltpu.roll(values, step % count, 0))


class Fabric:
    def __init__(self):
        self.row = lax.axis_index("row")
        self.ch = lax.axis_index("ch")
        self.core = lax.rem(self.ch, 2)
        self.z = self.ch // 2
        self.zs = lax.axis_size("ch") // 2
        x, y = lax.rem(self.row, 2), self.row // 2
        self.row_x = y * 2 + (1 - x)
        self.row_y = (1 - y) * 2 + x
        self.row_d = (1 - y) * 2 + (1 - x)
        self.twin = self.z * 2 + (1 - self.core)
        self.sent = []
        self.held = []

    def z_at(self, d):
        return lax.rem(self.z + d, self.zs)

    def ch_at(self, d):
        return self.z_at(d) * 2 + self.core

    def partners(self):
        out = [(self.row, self.ch_at(d)) for d in range(1, self.zs)]
        out += [(r, self.ch) for r in (self.row_x, self.row_y, self.row_d)]
        return out + [(self.row, self.twin)]

    def send(self, src, dst, send_sem, recv_sem, device):
        copy = pltpu.make_async_remote_copy(
            src_ref=src,
            dst_ref=dst,
            send_sem=send_sem,
            recv_sem=recv_sem,
            device_id=device,
            device_id_type=MESH,
        )
        copy.start()
        self.sent.append(copy)

    def arrived(self, dst, sem):
        pltpu.make_async_remote_copy(
            src_ref=dst,
            dst_ref=dst,
            send_sem=sem,
            recv_sem=sem,
            device_id=(self.row, self.twin),
            device_id_type=MESH,
        ).wait_recv()


class Gather:
    def __init__(self, fab, buf, recv, send_z, send_x, send_y, send_t):
        self.fab, self.buf, self.recv = fab, buf, recv
        self.send_z, self.send_x, self.send_y, self.send_t = send_z, send_x, send_y, send_t

    def push(self, k, r, send_sem, device):
        slot = self.buf.at[k, r]
        self.fab.send(slot, slot, send_sem, self.recv.at[k, r], device)

    def to_x(self, k, r, n):
        self.push(k, r, self.send_x.at[n], (self.fab.row_x, self.fab.ch))

    def to_y(self, k, r, n):
        self.push(k, r, self.send_y.at[n], (self.fab.row_y, self.fab.ch))

    def to_twin(self, k, r, n):
        self.push(k, r, self.send_t.at[n], (self.fab.row, self.fab.twin))

    def wait(self, k, r):
        self.fab.arrived(self.buf.at[k, r], self.recv.at[k, r])

    def start(self):
        f = self.fab
        self.relay(0, 1)
        self.relay(0, -1)
        self.to_x(f.ch, f.row, 0)
        self.to_y(f.ch, f.row, 0)
        self.to_twin(f.ch, f.row, 0)

    def relay(self, d, way):
        f = self.fab
        k = f.ch_at(d)
        slot = self.buf.at[k, f.row]
        sem = self.send_z.at[f.zs if d == 0 and way == 1 else d]

        def copy():
            return pltpu.make_async_remote_copy(
                src_ref=slot,
                dst_ref=slot,
                send_sem=sem,
                recv_sem=self.recv.at[k, f.row],
                device_id=(f.row, f.ch + 2 * way),
                device_id_type=MESH,
            )

        above = f.z + d < f.zs
        came = True if d == 0 else above if way == -1 else jnp.logical_not(above)
        more = f.z > 0 if way == -1 else f.z < f.zs - 1
        go = more if d == 0 else jnp.logical_and(came, more)

        @pl.when(go)
        def _():
            copy().start()

        f.held.append((go, copy))

    def land_z(self, step):
        f = self.fab
        for d, way in ((step, -1), (f.zs - step, 1)):
            here = f.z + d < f.zs if way == -1 else f.z + d >= f.zs

            @pl.when(here)
            def _():
                self.wait(f.ch_at(d), f.row)

            self.relay(d, way)

            @pl.when(here)
            def _():
                self.twin_copy(d).start()

    def twin_copy(self, d):
        f = self.fab
        slot = self.buf.at[f.ch_at(d), f.row]
        return pltpu.make_async_remote_copy(
            src_ref=slot,
            dst_ref=slot,
            send_sem=self.send_t.at[d],
            recv_sem=self.recv.at[f.ch_at(d), f.row],
            device_id=(f.row, f.twin),
            device_id_type=MESH,
        )

    def landed_z(self):
        for d in range(1, self.fab.zs):
            self.fab.sent.append(self.twin_copy(d))

    def spread_z(self, d):
        f = self.fab
        self.to_x(f.ch_at(d), f.row, d)
        self.to_y(f.ch_at(d), f.row, d)

    def pump_xy(self, d):
        f = self.fab
        half = f.zs // 2
        k = f.ch_at(d)
        self.wait(k, f.row_x)
        if d < half:
            self.to_y(k, f.row_x, f.zs + d)
        self.to_twin(k, f.row_x, f.zs + d)
        self.wait(k, f.row_y)
        if d >= half:
            self.to_x(k, f.row_y, f.zs + d - half)
        self.to_twin(k, f.row_y, 2 * f.zs + d)

    def pump_d(self, d):
        f = self.fab
        k = f.ch_at(d)
        self.wait(k, f.row_d)
        self.to_twin(k, f.row_d, 3 * f.zs + d)

    def from_twin(self, d, r):
        f = self.fab
        self.wait(f.z_at(d) * 2 + (1 - f.core), r)


class Scatter:
    def __init__(self, fab, give, got, out, far, acc, give_s, got_s, out_s, far_s):
        self.fab, self.give, self.got, self.out, self.far, self.acc = fab, give, got, out, far, acc
        self.give_s, self.got_s, self.out_s, self.far_s = give_s, got_s, out_s, far_s

    def part(self, lhs, w_ref, k):
        width = lhs.shape[1]
        rows = pl.ds(pl.multiple_of(k * width, width), width)
        return dot_nt(lhs, w_ref[rows, :])

    def start(self, lhs, w_ref):
        f = self.fab
        for d in (1, 2, 3, 0):
            at = f.z_at(d)
            self.give[at] = self.part(lhs, w_ref, at * 2 + (1 - f.core)).astype(BF)
            f.send(
                self.give.at[at],
                self.got.at[at],
                self.give_s.at[d],
                self.got_s.at[at],
                (f.row, f.twin),
            )

    def middle(self, lhs, w_ref):
        f = self.fab
        for d in (1, 2, 3, 0):
            at = f.z_at(d)
            own = self.part(lhs, w_ref, at * 2 + f.core)
            f.arrived(self.got.at[at], self.got_s.at[at])
            own = own + self.got[at].astype(F32)
            if d == 0:
                self.acc[...] = own
            else:
                self.out[at] = own.astype(BF)
                f.send(
                    self.out.at[at],
                    self.far.at[f.z],
                    self.out_s.at[d - 1],
                    self.far_s.at[f.z],
                    (f.row, f.ch_at(d)),
                )

    def finish(self):
        f = self.fab
        for d in (1, 2, 3):
            at = f.z_at(d)
            f.arrived(self.far.at[at], self.far_s.at[at])
        total = self.acc[...]
        for d in (1, 2, 3):
            total = total + self.far[f.z_at(d)].astype(F32)
        return total


def block_kernel(*refs):
    (feat, w_in_hbm, wg, w_out_hbm, cot, out, g_in, gw_in, gw_group, gw_out) = refs[:10]
    (b1, b2, w_in, w_out, pre, act, gt, g1, cots, shifted, wide, stage) = refs[10:22]
    (r1, z1, x1, y1, t1, r2, z2, x2, y2, t2) = refs[22:32]
    s1, s2 = refs[32:41], refs[41:50]
    cot_send, cot_recv, gt_send, gt_recv, halo_send, halo_recv, local = refs[50:57]
    fab = Fabric()
    rows = cots.shape[0]
    pixels, width = feat.shape
    chunk = wide.shape[2]
    gw = wg.shape[1]
    count_k = b1.shape[0]
    chunks = [slice(i * chunk, (i + 1) * chunk) for i in range(width // chunk)]

    load_out = pltpu.make_async_copy(w_out_hbm, w_out, local.at[0])
    load_in = pltpu.make_async_copy(w_in_hbm, w_in, local.at[1])
    load_out.start()
    load_in.start()
    barrier = pltpu.get_barrier_semaphore()
    partners = fab.partners()
    for device in partners:
        pl.semaphore_signal(barrier, inc=1, device_id=device, device_id_type=MESH)
    pl.semaphore_wait(barrier, len(partners))

    gather1 = Gather(fab, b1, r1, z1, x1, y1, t1)
    gather2 = Gather(fab, b2, r2, z2, x2, y2, t2)
    scatter1 = Scatter(fab, *s1)
    scatter2 = Scatter(fab, *s2)
    other_rows = (fab.row_x, fab.row_y, fab.row_d)

    b1[fab.ch, fab.row] = feat[...]
    gather1.start()
    cots[fab.row] = cot[...]
    for n, r in enumerate(other_rows):
        fab.send(
            cots.at[fab.row],
            cots.at[fab.row],
            cot_send.at[n],
            cot_recv.at[fab.row],
            (r, fab.ch),
        )
    load_out.wait()
    scatter1.start(cot[...], w_out)

    blank = jnp.zeros((pixels, width), BF)
    act[0] = blank
    act[rows + 1] = blank
    gt[0] = blank
    gt[rows + 1] = blank
    row_group = lax.broadcasted_iota(jnp.int32, (chunk, chunk), 0) // gw
    col_group = lax.broadcasted_iota(jnp.int32, (chunk, chunk), 1) // gw
    same = row_group == col_group

    def widen(tap, carry):
        for i, part in enumerate(chunks):
            taps = wg[tap, :, part].astype(F32)
            dense = jnp.concatenate([taps] * (chunk // gw), axis=0)
            wide[tap, i] = jnp.where(same, dense, 0.0).astype(BF)
        return carry

    lax.fori_loop(0, 9, widen, 0)

    depths = range(fab.zs)
    load_in.wait()

    def activate(r):
        value = pre[r]
        act[r + 1] = (value * jax.nn.sigmoid(value)).astype(BF)

    def first_xy(d):
        for r in (fab.row_x, fab.row_y):
            gather1.from_twin(d, r)

        def add(i, carry):
            r = fab.row_x + lax.rem(i, 2) * (fab.row_y - fab.row_x)
            k = fab.z_at(d) * 2 + i // 2
            lines = pl.ds(pl.multiple_of(k * width, width), width)
            pre[r] += dot(b1[k, r], w_in[lines, :])
            return carry

        lax.fori_loop(0, 4, add, 0)

    def first(r):
        for d in depths:
            gather1.from_twin(d, r)
        pre[r] = jnp.zeros((pixels, width), F32)

        def add(k, carry):
            lines = pl.ds(pl.multiple_of(k * width, width), width)
            pre[r] += dot(b1[k, r], w_in[lines, :])
            return carry

        lax.fori_loop(0, count_k, add, 0)
        activate(r)

    for d in depths[1:]:
        gather1.land_z(d)
    gather1.landed_z()
    first(fab.row)
    above, below = fab.row > 0, fab.row < rows - 1

    def halo(n, r):
        return pltpu.make_async_remote_copy(
            src_ref=act.at[fab.row + 1],
            dst_ref=act.at[fab.row + 1],
            send_sem=halo_send.at[n],
            recv_sem=halo_recv.at[n],
            device_id=(r, fab.ch),
            device_id_type=MESH,
        )

    def halo_from(n, r):
        return pltpu.make_async_remote_copy(
            src_ref=act.at[r + 1],
            dst_ref=act.at[r + 1],
            send_sem=halo_send.at[n],
            recv_sem=halo_recv.at[n],
            device_id=(r, fab.ch),
            device_id_type=MESH,
        )

    @pl.when(above)
    def _():
        halo(0, fab.row - 1).start()

    @pl.when(below)
    def _():
        halo(1, fab.row + 1).start()

    for d in depths[1:]:
        gather1.spread_z(d)
    scatter1.middle(cot[...], w_out)

    @pl.when(above)
    def _():
        halo(0, fab.row - 1).wait_send()
        halo_from(1, fab.row - 1).wait_recv()

    @pl.when(below)
    def _():
        halo(1, fab.row + 1).wait_send()
        halo_from(0, fab.row + 1).wait_recv()

    taps_of = [[a * 3 + b for a in range(3)] for b in range(3)]
    two = []
    for i, part in enumerate(chunks):
        total = None
        for b in range(3):
            side = None
            for a in range(3):
                term = dot(act[fab.row + a, :, part], wide[taps_of[b][a], i])
                side = term if side is None else side + term
            side = moved(side, 1) if b == 0 else moved(side, -1) if b == 2 else side
            total = side if total is None else total + side
        two.append(total)
    slopes = []
    for i, part in enumerate(chunks):
        b2[fab.ch, fab.row, part, :] = (two[i] * jax.nn.sigmoid(two[i])).T.astype(BF)
        slopes.append(silu_slope(two[i]))
    gather2.start()
    pre[fab.row_x] = jnp.zeros((pixels, width), F32)
    pre[fab.row_y] = jnp.zeros((pixels, width), F32)
    gather1.pump_xy(0)
    gather1.pump_xy(1)
    first_xy(0)
    gather2.land_z(1)
    gather1.pump_xy(2)
    first_xy(1)
    gather2.land_z(2)
    gather1.pump_xy(3)
    first_xy(2)
    d_two = scatter1.finish()
    for i, part in enumerate(chunks):
        gt[fab.row + 1, :, part] = (d_two[:, part] * slopes[i]).astype(BF)
    for n, r in enumerate(other_rows):
        fab.send(
            gt.at[fab.row + 1],
            gt.at[fab.row + 1],
            gt_send.at[n],
            gt_recv.at[fab.row],
            (r, fab.ch),
        )
    first_xy(3)
    gather2.land_z(3)
    gather2.landed_z()
    for d in depths[1:]:
        gather2.spread_z(d)
    for d in depths:
        gather1.pump_d(d)
    activate(fab.row_x)
    activate(fab.row_y)
    first(fab.row_d)
    for r in other_rows:
        fab.arrived(gt.at[r + 1], gt_recv.at[r])

    def back(q, carry):
        for i, part in enumerate(chunks):
            total = None
            for b in range(3):
                side = None
                for a in range(3):
                    term = dot_nt(gt[q + 2 - a, :, part], wide[taps_of[b][a], i])
                    side = term if side is None else side + term
                side = moved(side, -1) if b == 0 else moved(side, 1) if b == 2 else side
                total = side if total is None else total + side
            g1[q, :, part] = (total * silu_slope(pre[q, :, part])).astype(BF)
        return carry

    lax.fori_loop(0, rows, back, 0)
    scatter2.start(g1[fab.row], w_in)
    scatter2.middle(g1[fab.row], w_in)

    for d in depths:
        gather2.from_twin(d, fab.row)
    pre[0] = feat[...].astype(F32)

    def last(k, carry):
        lines = pl.ds(pl.multiple_of(k * width, width), width)
        pre[0] += dot_tn(b2[k, fab.row], w_out[lines, :])
        return carry

    lax.fori_loop(0, count_k, last, 0)
    out[...] = pre[0].astype(BF)

    def product_in(k):
        left = b1[k].reshape(rows * pixels, width)
        return dot_tn(left, g1[...].reshape(rows * pixels, width))

    def product_out(k):
        left = jnp.concatenate([b2[k, r] for r in range(rows)], axis=1)
        return dot(left, cots[...].reshape(rows * pixels, width))

    def weight_grad(product, result, sems, d):
        def store(slot):
            k = fab.z_at(d) * 2 + slot
            return pltpu.make_async_copy(
                stage.at[slot],
                result.at[pl.ds(pl.multiple_of(k * width, width), width), :],
                sems.at[slot],
            )

        def step(slot, carry):
            full = product(fab.z_at(d) * 2 + slot).astype(BF)
            if d > 0:
                store(slot).wait()
            stage[slot] = full
            store(slot).start()
            return carry

        lax.fori_loop(0, 2, step, 0)
        if d == fab.zs - 1:
            for slot in range(2):
                store(slot).wait()

    for d in depths:
        weight_grad(product_in, gw_in, local.at[pl.ds(2, 2)], d)
        gather2.pump_xy(d)

    for b in range(3):

        def move(q, carry):
            value = gt[q + 1].astype(F32)
            value = moved(value, -1) if b == 0 else moved(value, 1) if b == 2 else value
            shifted[q] = value.astype(BF)
            return carry

        lax.fori_loop(0, rows, move, 0)

        def tap_grad(a, carry):
            for part in chunks:
                lhs = act[pl.ds(a, rows), :, part].reshape(rows * pixels, chunk)
                full = dot_tn(lhs, shifted[:, :, part].reshape(rows * pixels, chunk))
                full = jnp.where(same, full, 0.0).reshape(chunk // gw, gw, chunk)
                gw_group[a * 3 + b, :, part] = jnp.sum(full, axis=0).astype(BF)
            return carry

        lax.fori_loop(0, 3, tap_grad, 0)

    for r in other_rows:
        fab.arrived(cots.at[r], cot_recv.at[r])
    for d in depths:
        gather2.pump_d(d)
        for r in other_rows:
            gather2.from_twin(d, r)
        weight_grad(product_out, gw_out, local.at[pl.ds(4, 2)], d)
    g_in[...] = (cot[...].astype(F32) + scatter2.finish()).astype(BF)
    for copy in fab.sent:
        copy.wait_send()
    for go, copy in fab.held:

        @pl.when(go)
        def _():
            copy().wait_send()


def hand_over(*refs):
    sources, results, held = refs[:5], refs[5:10], refs[10:15]
    load_sems, store_sems = refs[15:]
    loads, stores = [], []
    for n, (src, mid, dst) in enumerate(zip(sources, held, results)):
        parts = 4 if src.shape[0] % 1024 == 0 else 1
        size = src.shape[0] // parts
        for p in range(parts):
            rows = pl.ds(p * size, size)
            loads.append(pltpu.make_async_copy(src.at[rows], mid.at[rows], load_sems.at[n, p]))
            stores.append(pltpu.make_async_copy(mid.at[rows], dst.at[rows], store_sems.at[n, p]))
    for load in loads:
        load.start()
    for load, store in zip(loads, stores):
        load.wait()
        store.start()
    for store in stores:
        store.wait()


def body(features, w_in, w_group, w_out, cotangent):
    row_count, pixels, width = features.shape
    rows, lanes = lax.axis_size("row"), lax.axis_size("ch")
    total = rows * lanes * features.size * features.dtype.itemsize
    fits = (rows, lanes, row_count) == (4, 8, 1) and w_in.shape[1] == width == 512
    if not fits or total > GATHER_BYTES:
        return wide_body(features, w_in, w_group, w_out, cotangent)
    zs = lanes // 2
    channels = w_in.shape[0]
    gw = w_group.shape[2]
    dma = pltpu.SemaphoreType.DMA
    vmem = pltpu.VMEM
    gather_sems = [dma((lanes, rows)), dma((zs + 1,)), dma((6,)), dma((6,)), dma((rows * zs,))]
    part = vmem((zs, pixels, width), BF)
    scatter = [part, part, part, part, vmem((pixels, width), F32)]
    scatter += [dma((zs,)), dma((zs,)), dma((zs - 1,)), dma((zs,))]
    scratch = [
        vmem((lanes, rows, pixels, width), BF),
        vmem((lanes, rows, width, pixels), BF),
        vmem((channels, width), BF),
        vmem((channels, width), BF),
        vmem((rows, pixels, width), F32),
        vmem((rows + 2, pixels, width), BF),
        vmem((rows + 2, pixels, width), BF),
        vmem((rows, pixels, width), BF),
        vmem((rows, pixels, width), BF),
        vmem((rows, pixels, width), BF),
        vmem((9, width // 256, 256, 256), BF),
        vmem((2, width, width), BF),
    ]
    scratch += gather_sems * 2 + scatter * 2
    scratch += [dma((3,)), dma((rows,)), dma((3,)), dma((rows,)), dma((2,)), dma((2,)), dma((6,))]
    in_vmem = pl.BlockSpec(memory_space=pltpu.VMEM)
    in_any = pl.BlockSpec(memory_space=pl.ANY)
    flat = jax.ShapeDtypeStruct((pixels, width), BF)
    weight = jax.ShapeDtypeStruct((channels, width), BF)
    results = pl.pallas_call(
        block_kernel,
        out_shape=[flat, flat, weight, jax.ShapeDtypeStruct((9, gw, width), BF), weight],
        in_specs=[in_vmem, in_any, in_vmem, in_any, in_vmem],
        out_specs=[in_vmem, in_vmem, in_any, in_vmem, in_any],
        scratch_shapes=scratch,
        compiler_params=pltpu.CompilerParams(
            collective_id=0, has_side_effects=True, vmem_limit_bytes=60 * 1024 * 1024
        ),
    )(
        features.reshape(pixels, width),
        w_in,
        w_group.reshape(9, gw, width),
        w_out,
        cotangent.reshape(pixels, width),
    )
    out, g_in, gw_in, gw_group, gw_out = pl.pallas_call(
        hand_over,
        out_shape=[jax.ShapeDtypeStruct(v.shape, v.dtype) for v in results],
        in_specs=[in_any] * 5,
        out_specs=[in_any] * 5,
        scratch_shapes=[vmem(v.shape, v.dtype) for v in results] + [dma((5, 4)), dma((5, 4))],
        compiler_params=pltpu.CompilerParams(vmem_limit_bytes=60 * 1024 * 1024),
    )(*results)
    return (
        out.reshape(features.shape),
        g_in.reshape(features.shape),
        gw_in,
        gw_group.reshape(w_group.shape),
        gw_out,
    )


def solution(mesh):
    placed = (
        P("row", None, "ch"),
        P(None, "ch"),
        P(None, None, None, "ch"),
        P(None, "ch"),
        P("row", None, "ch"),
    )
    return jax.shard_map(
        body,
        mesh=mesh,
        in_specs=placed,
        out_specs=(
            P("row", None, "ch"),
            P("row", None, "ch"),
            P(None, "ch"),
            P(None, None, None, "ch"),
            P(None, "ch"),
        ),
        check_vma=False,
    )
```

```python
import jax
import jax.numpy as jnp
from jax import lax
from jax.experimental import pallas as pl
from jax.experimental.pallas import tpu as pltpu
from jax.sharding import PartitionSpec as P


GATHER_BYTES = 8 * 1024 * 1024
MESH = pl.DeviceIdType.MESH
BF = jnp.bfloat16
F32 = jnp.float32


def padded_2(cells, sides, width):
    for axis, dim in sides:
        count = lax.axis_size(axis)
        ends = count - 1
        head = lax.slice_in_dim(cells, 0, width, axis=dim)
        tail = lax.slice_in_dim(cells, cells.shape[dim] - width, cells.shape[dim], axis=dim)
        cells = jnp.concatenate(
            [
                lax.ppermute(tail, axis, [(i, (i + 1) % count) for i in range(ends)]),
                cells,
                lax.ppermute(head, axis, [((i + 1) % count, i) for i in range(ends)]),
            ],
            axis=dim,
        )
    return cells


def silu_slope(values):
    sigma = jax.nn.sigmoid(values)
    return sigma * (1.0 + values * (1.0 - sigma))


def full_channels(local):
    return lax.all_gather(local, "ch", axis=2, tiled=True)


def row_rims(local):
    padded = padded_2(local, (("row", 0),), 1)
    return jnp.pad(padded, ((0, 0), (1, 1), (0, 0)))


def group_view(local, group_width):
    return local.reshape(local.shape[0], local.shape[1], local.shape[2] // group_width, group_width)


def wide_body(features, w_in, w_group, w_out, cotangent):
    row_count, col_count, local_ch = features.shape
    group_width = w_group.shape[2]
    local_mid = w_in.shape[1]
    pixel_count = row_count * col_count
    gathered = full_channels(features)
    flat_in = gathered.reshape(pixel_count, -1)
    pre_one = jnp.dot(flat_in, w_in, preferred_element_type=jnp.float32)
    act_one = jax.nn.silu(pre_one).astype(jnp.bfloat16).reshape(row_count, col_count, local_mid)
    padded_one = group_view(row_rims(act_one), group_width)
    filters = w_group.reshape(3, 3, group_width, local_mid // group_width, group_width)
    pre_two = jnp.zeros((row_count, col_count, local_mid // group_width, group_width), jnp.float32)
    for row_tap in range(3):
        for col_tap in range(3):
            window = padded_one[row_tap : row_tap + row_count, col_tap : col_tap + col_count]
            pre_two = pre_two + jnp.einsum(
                "rcgi,igj->rcgj",
                window,
                filters[row_tap, col_tap],
                preferred_element_type=jnp.float32,
            )
    pre_two = pre_two.reshape(pixel_count, local_mid)
    act_two = jax.nn.silu(pre_two).astype(jnp.bfloat16)
    mid_full = full_channels(act_two.reshape(row_count, col_count, local_mid)).reshape(
        pixel_count, -1
    )
    branch = jnp.dot(mid_full, w_out, preferred_element_type=jnp.float32)
    flat_local = features.reshape(pixel_count, local_ch)
    block_out = (
        (flat_local.astype(jnp.float32) + branch)
        .astype(jnp.bfloat16)
        .reshape(row_count, col_count, local_ch)
    )
    grad_flat = cotangent.reshape(pixel_count, local_ch)
    partial = lax.dot_general(
        w_out, grad_flat, (((1,), (1,)), ((), ())), preferred_element_type=jnp.float32
    ).astype(jnp.bfloat16)
    d_two = (
        lax.psum_scatter(partial, "ch", scatter_dimension=0, tiled=True).astype(jnp.float32).T
    )
    grad_two = (d_two * silu_slope(pre_two)).astype(jnp.bfloat16)
    padded_two = group_view(
        row_rims(grad_two.reshape(row_count, col_count, local_mid)), group_width
    )
    d_one = jnp.zeros((row_count, col_count, local_mid // group_width, group_width), jnp.float32)
    for row_tap in range(3):
        for col_tap in range(3):
            window = padded_two[
                2 - row_tap : 2 - row_tap + row_count, 2 - col_tap : 2 - col_tap + col_count
            ]
            d_one = d_one + jnp.einsum(
                "rcgj,igj->rcgi",
                window,
                filters[row_tap, col_tap],
                preferred_element_type=jnp.float32,
            )
    grad_one = (d_one.reshape(pixel_count, local_mid) * silu_slope(pre_one)).astype(jnp.bfloat16)
    grad_view = group_view(grad_two.reshape(row_count, col_count, local_mid), group_width)
    tap_rows = []
    for row_tap in range(3):
        tap_line = []
        for col_tap in range(3):
            window = padded_one[row_tap : row_tap + row_count, col_tap : col_tap + col_count]
            tap_line.append(
                jnp.einsum("rcgi,rcgj->igj", window, grad_view, preferred_element_type=jnp.float32)
            )
        tap_rows.append(jnp.stack(tap_line))
    group_grad = jnp.stack(tap_rows).reshape(3, 3, group_width, local_mid)
    rows = lax.axis_size("row")
    spread = rows * flat_in.size * flat_in.dtype.itemsize <= GATHER_BYTES
    left_in, right_in, left_out, right_out = flat_in, grad_one, mid_full, grad_flat
    if spread:
        left_in, right_in, left_out, right_out = (
            lax.all_gather(v, "row", axis=0, tiled=True)
            for v in (flat_in, grad_one, mid_full, grad_flat)
        )
    in_grad = lax.dot_general(
        left_in, right_in, (((0,), (0,)), ((), ())), preferred_element_type=jnp.float32
    ).astype(jnp.bfloat16)
    out_grad = lax.dot_general(
        left_out, right_out, (((0,), (0,)), ((), ())), preferred_element_type=jnp.float32
    ).astype(jnp.bfloat16)
    if not spread:
        in_grad, out_grad = lax.psum((in_grad, out_grad), "row")
    d_input = (
        lax.psum_scatter(
            lax.dot_general(
                w_in, grad_one, (((1,), (1,)), ((), ())), preferred_element_type=jnp.float32
            ).astype(jnp.bfloat16),
            "ch",
            scatter_dimension=0,
            tiled=True,
        )
        .astype(jnp.float32)
        .T
    )
    grad_input = (
        (grad_flat.astype(jnp.float32) + d_input)
        .astype(jnp.bfloat16)
        .reshape(row_count, col_count, local_ch)
    )
    group_grad = lax.psum(group_grad.astype(jnp.bfloat16), "row")
    return block_out, grad_input, in_grad, group_grad, out_grad


def dot(a, b):
    return jnp.dot(a, b, preferred_element_type=F32)


def dot_nt(a, b):
    return lax.dot_general(a, b, (((1,), (1,)), ((), ())), preferred_element_type=F32)


def dot_tn(a, b):
    return lax.dot_general(a, b, (((0,), (0,)), ((), ())), preferred_element_type=F32)


def moved(values, step):
    count = values.shape[0]
    at = lax.broadcasted_iota(jnp.int32, values.shape, 0)
    edge = 0 if step == 1 else count - 1
    return jnp.where(at == edge, 0.0, pltpu.roll(values, step % count, 0))


class Fabric:
    def __init__(self):
        self.row = lax.axis_index("row")
        self.ch = lax.axis_index("ch")
        self.core = lax.rem(self.ch, 2)
        self.z = self.ch // 2
        self.zs = lax.axis_size("ch") // 2
        x, y = lax.rem(self.row, 2), self.row // 2
        self.row_x = y * 2 + (1 - x)
        self.row_y = (1 - y) * 2 + x
        self.row_d = (1 - y) * 2 + (1 - x)
        self.twin = self.z * 2 + (1 - self.core)
        self.sent = []
        self.held = []

    def z_at(self, d):
        return lax.rem(self.z + d, self.zs)

    def ch_at(self, d):
        return self.z_at(d) * 2 + self.core

    def partners(self):
        out = [(self.row, self.ch_at(d)) for d in range(1, self.zs)]
        out += [(r, self.ch) for r in (self.row_x, self.row_y, self.row_d)]
        return out + [(self.row, self.twin)]

    def send(self, src, dst, send_sem, recv_sem, device):
        copy = pltpu.make_async_remote_copy(
            src_ref=src,
            dst_ref=dst,
            send_sem=send_sem,
            recv_sem=recv_sem,
            device_id=device,
            device_id_type=MESH,
        )
        copy.start()
        self.sent.append(copy)

    def arrived(self, dst, sem):
        pltpu.make_async_remote_copy(
            src_ref=dst,
            dst_ref=dst,
            send_sem=sem,
            recv_sem=sem,
            device_id=(self.row, self.twin),
            device_id_type=MESH,
        ).wait_recv()


class Gather:
    def __init__(self, fab, buf, recv, send_z, send_x, send_y, send_t):
        self.fab, self.buf, self.recv = fab, buf, recv
        self.send_z, self.send_x, self.send_y, self.send_t = send_z, send_x, send_y, send_t

    def push(self, k, r, send_sem, device):
        slot = self.buf.at[k, r]
        self.fab.send(slot, slot, send_sem, self.recv.at[k, r], device)

    def to_x(self, k, r, n):
        self.push(k, r, self.send_x.at[n], (self.fab.row_x, self.fab.ch))

    def to_y(self, k, r, n):
        self.push(k, r, self.send_y.at[n], (self.fab.row_y, self.fab.ch))

    def to_twin(self, k, r, n):
        self.push(k, r, self.send_t.at[n], (self.fab.row, self.fab.twin))

    def wait(self, k, r):
        self.fab.arrived(self.buf.at[k, r], self.recv.at[k, r])

    def start(self):
        f = self.fab
        self.relay(0, 1)
        self.relay(0, -1)
        self.to_x(f.ch, f.row, 0)
        self.to_y(f.ch, f.row, 0)
        self.to_twin(f.ch, f.row, 0)

    def relay(self, d, way):
        f = self.fab
        k = f.ch_at(d)
        slot = self.buf.at[k, f.row]
        sem = self.send_z.at[f.zs if d == 0 and way == 1 else d]

        def copy():
            return pltpu.make_async_remote_copy(
                src_ref=slot,
                dst_ref=slot,
                send_sem=sem,
                recv_sem=self.recv.at[k, f.row],
                device_id=(f.row, f.ch + 2 * way),
                device_id_type=MESH,
            )

        above = f.z + d < f.zs
        came = True if d == 0 else above if way == -1 else jnp.logical_not(above)
        more = f.z > 0 if way == -1 else f.z < f.zs - 1
        go = more if d == 0 else jnp.logical_and(came, more)

        @pl.when(go)
        def _():
            copy().start()

        f.held.append((go, copy))

    def land_z(self, step):
        f = self.fab
        for d, way in ((step, -1), (f.zs - step, 1)):
            here = f.z + d < f.zs if way == -1 else f.z + d >= f.zs

            @pl.when(here)
            def _():
                self.wait(f.ch_at(d), f.row)

            self.relay(d, way)

            @pl.when(here)
            def _():
                self.twin_copy(d).start()

    def twin_copy(self, d):
        f = self.fab
        slot = self.buf.at[f.ch_at(d), f.row]
        return pltpu.make_async_remote_copy(
            src_ref=slot,
            dst_ref=slot,
            send_sem=self.send_t.at[d],
            recv_sem=self.recv.at[f.ch_at(d), f.row],
            device_id=(f.row, f.twin),
            device_id_type=MESH,
        )

    def landed_z(self):
        for d in range(1, self.fab.zs):
            self.fab.sent.append(self.twin_copy(d))

    def spread_z(self, d):
        f = self.fab
        self.to_x(f.ch_at(d), f.row, d)
        self.to_y(f.ch_at(d), f.row, d)

    def pump_xy(self, d):
        f = self.fab
        half = f.zs // 2
        k = f.ch_at(d)
        self.wait(k, f.row_x)
        if d < half:
            self.to_y(k, f.row_x, f.zs + d)
        self.to_twin(k, f.row_x, f.zs + d)
        self.wait(k, f.row_y)
        if d >= half:
            self.to_x(k, f.row_y, f.zs + d - half)
        self.to_twin(k, f.row_y, 2 * f.zs + d)

    def pump_d(self, d):
        f = self.fab
        k = f.ch_at(d)
        self.wait(k, f.row_d)
        self.to_twin(k, f.row_d, 3 * f.zs + d)

    def from_twin(self, d, r):
        f = self.fab
        self.wait(f.z_at(d) * 2 + (1 - f.core), r)


class Scatter:
    def __init__(self, fab, give, got, out, far, acc, give_s, got_s, out_s, far_s):
        self.fab, self.give, self.got, self.out, self.far, self.acc = fab, give, got, out, far, acc
        self.give_s, self.got_s, self.out_s, self.far_s = give_s, got_s, out_s, far_s

    def part(self, lhs, w_ref, k):
        width = lhs.shape[1]
        rows = pl.ds(pl.multiple_of(k * width, width), width)
        return dot_nt(lhs, w_ref[rows, :])

    def start(self, lhs, w_ref):
        f = self.fab
        for d in (1, 2, 3, 0):
            at = f.z_at(d)
            self.give[at] = self.part(lhs, w_ref, at * 2 + (1 - f.core)).astype(BF)
            f.send(
                self.give.at[at],
                self.got.at[at],
                self.give_s.at[d],
                self.got_s.at[at],
                (f.row, f.twin),
            )

    def middle(self, lhs, w_ref):
        f = self.fab
        for d in (1, 2, 3, 0):
            at = f.z_at(d)
            own = self.part(lhs, w_ref, at * 2 + f.core)
            f.arrived(self.got.at[at], self.got_s.at[at])
            own = own + self.got[at].astype(F32)
            if d == 0:
                self.acc[...] = own
            else:
                self.out[at] = own.astype(BF)
                f.send(
                    self.out.at[at],
                    self.far.at[f.z],
                    self.out_s.at[d - 1],
                    self.far_s.at[f.z],
                    (f.row, f.ch_at(d)),
                )

    def finish(self):
        f = self.fab
        for d in (1, 2, 3):
            at = f.z_at(d)
            f.arrived(self.far.at[at], self.far_s.at[at])
        total = self.acc[...]
        for d in (1, 2, 3):
            total = total + self.far[f.z_at(d)].astype(F32)
        return total


def block_kernel(*refs):
    (feat, w_in_hbm, wg, w_out_hbm, cot, out, g_in, gw_in, gw_group, mids, cot_rows) = refs[:11]
    refs = refs[1:]
    (b1, b2, w_in, w_out, pre, act, gt, g1, cots, shifted, wide, stage) = refs[10:22]
    act_t = refs[57]
    (r1, z1, x1, y1, t1, r2, z2, x2, y2, t2) = refs[22:32]
    s1, s2 = refs[32:41], refs[41:50]
    cot_send, cot_recv, gt_send, gt_recv, halo_send, halo_recv, local = refs[50:57]
    fab = Fabric()
    rows = cots.shape[0]
    pixels, width = feat.shape
    chunk = wide.shape[2]
    gw = wg.shape[1]
    count_k = b1.shape[0]
    chunks = [slice(i * chunk, (i + 1) * chunk) for i in range(width // chunk)]

    load_out = pltpu.make_async_copy(w_out_hbm, w_out, local.at[0])
    load_in = pltpu.make_async_copy(w_in_hbm, w_in, local.at[1])
    load_out.start()
    load_in.start()
    barrier = pltpu.get_barrier_semaphore()
    partners = fab.partners()
    for device in partners:
        pl.semaphore_signal(barrier, inc=1, device_id=device, device_id_type=MESH)
    pl.semaphore_wait(barrier, len(partners))

    gather1 = Gather(fab, b1, r1, z1, x1, y1, t1)
    gather2 = Gather(fab, b2, r2, z2, x2, y2, t2)
    scatter1 = Scatter(fab, *s1)
    scatter2 = Scatter(fab, *s2)
    other_rows = (fab.row_x, fab.row_y, fab.row_d)

    b1[fab.ch, fab.row] = feat[...]
    gather1.start()
    cots[fab.row] = cot[...]
    for n, r in enumerate(other_rows):
        fab.send(
            cots.at[fab.row],
            cots.at[fab.row],
            cot_send.at[n],
            cot_recv.at[fab.row],
            (r, fab.ch),
        )
    load_out.wait()
    scatter1.start(cot[...], w_out)

    blank = jnp.zeros((pixels, width), BF)
    act[0] = blank
    act[rows + 1] = blank
    gt[0] = blank
    gt[rows + 1] = blank
    row_group = lax.broadcasted_iota(jnp.int32, (chunk, chunk), 0) // gw
    col_group = lax.broadcasted_iota(jnp.int32, (chunk, chunk), 1) // gw
    same = row_group == col_group

    def widen(tap, carry):
        for i, part in enumerate(chunks):
            taps = wg[tap, :, part].astype(F32)
            dense = jnp.concatenate([taps] * (chunk // gw), axis=0)
            wide[tap, i] = jnp.where(same, dense, 0.0).astype(BF)
        return carry

    lax.fori_loop(0, 9, widen, 0)

    depths = range(fab.zs)
    load_in.wait()

    def activate(r):
        value = pre[r]
        act[r + 1] = (value * jax.nn.sigmoid(value)).astype(BF)

    def first_xy(d):
        for r in (fab.row_x, fab.row_y):
            gather1.from_twin(d, r)

        def add(i, carry):
            r = fab.row_x + lax.rem(i, 2) * (fab.row_y - fab.row_x)
            k = fab.z_at(d) * 2 + i // 2
            lines = pl.ds(pl.multiple_of(k * width, width), width)
            pre[r] += dot(b1[k, r], w_in[lines, :])
            return carry

        lax.fori_loop(0, 4, add, 0)

    def first(r):
        for d in depths:
            gather1.from_twin(d, r)
        pre[r] = jnp.zeros((pixels, width), F32)

        def add(k, carry):
            lines = pl.ds(pl.multiple_of(k * width, width), width)
            pre[r] += dot(b1[k, r], w_in[lines, :])
            return carry

        lax.fori_loop(0, count_k, add, 0)
        activate(r)

    for d in depths[1:]:
        gather1.land_z(d)
    gather1.landed_z()
    first(fab.row)
    above, below = fab.row > 0, fab.row < rows - 1

    def halo(n, r):
        return pltpu.make_async_remote_copy(
            src_ref=act.at[fab.row + 1],
            dst_ref=act.at[fab.row + 1],
            send_sem=halo_send.at[n],
            recv_sem=halo_recv.at[n],
            device_id=(r, fab.ch),
            device_id_type=MESH,
        )

    def halo_from(n, r):
        return pltpu.make_async_remote_copy(
            src_ref=act.at[r + 1],
            dst_ref=act.at[r + 1],
            send_sem=halo_send.at[n],
            recv_sem=halo_recv.at[n],
            device_id=(r, fab.ch),
            device_id_type=MESH,
        )

    @pl.when(above)
    def _():
        halo(0, fab.row - 1).start()

    @pl.when(below)
    def _():
        halo(1, fab.row + 1).start()

    for d in depths[1:]:
        gather1.spread_z(d)
    scatter1.middle(cot[...], w_out)

    @pl.when(above)
    def _():
        halo(0, fab.row - 1).wait_send()
        halo_from(1, fab.row - 1).wait_recv()

    @pl.when(below)
    def _():
        halo(1, fab.row + 1).wait_send()
        halo_from(0, fab.row + 1).wait_recv()

    taps_of = [[a * 3 + b for a in range(3)] for b in range(3)]
    two = []
    for i, part in enumerate(chunks):
        total = None
        for b in range(3):
            side = None
            for a in range(3):
                term = dot(act[fab.row + a, :, part], wide[taps_of[b][a], i])
                side = term if side is None else side + term
            side = moved(side, 1) if b == 0 else moved(side, -1) if b == 2 else side
            total = side if total is None else total + side
        two.append(total)
    slopes = []
    for i, part in enumerate(chunks):
        b2[fab.ch, fab.row, part, :] = (two[i] * jax.nn.sigmoid(two[i])).T.astype(BF)
        slopes.append(silu_slope(two[i]))
    gather2.start()
    pre[fab.row_x] = jnp.zeros((pixels, width), F32)
    pre[fab.row_y] = jnp.zeros((pixels, width), F32)
    gather1.pump_xy(0)
    gather1.pump_xy(1)
    first_xy(0)
    gather2.land_z(1)
    gather1.pump_xy(2)
    first_xy(1)
    gather2.land_z(2)
    gather1.pump_xy(3)
    first_xy(2)
    d_two = scatter1.finish()
    for i, part in enumerate(chunks):
        gt[fab.row + 1, :, part] = (d_two[:, part] * slopes[i]).astype(BF)
    for n, r in enumerate(other_rows):
        fab.send(
            gt.at[fab.row + 1],
            gt.at[fab.row + 1],
            gt_send.at[n],
            gt_recv.at[fab.row],
            (r, fab.ch),
        )
    first_xy(3)
    gather2.land_z(3)
    gather2.landed_z()
    for d in depths[1:]:
        gather2.spread_z(d)
    for d in depths:
        gather1.pump_d(d)
    activate(fab.row_x)
    activate(fab.row_y)
    first(fab.row_d)
    for r in other_rows:
        fab.arrived(gt.at[r + 1], gt_recv.at[r])

    def back(q, carry):
        for i, part in enumerate(chunks):
            total = None
            for b in range(3):
                side = None
                for a in range(3):
                    term = dot_nt(gt[q + 2 - a, :, part], wide[taps_of[b][a], i])
                    side = term if side is None else side + term
                side = moved(side, -1) if b == 0 else moved(side, 1) if b == 2 else side
                total = side if total is None else total + side
            g1[q, :, part] = (total * silu_slope(pre[q, :, part])).astype(BF)
        return carry

    lax.fori_loop(0, rows, back, 0)
    scatter2.start(g1[fab.row], w_in)
    scatter2.middle(g1[fab.row], w_in)

    for d in depths:
        gather2.from_twin(d, fab.row)
    pre[0] = feat[...].astype(F32)

    def last(k, carry):
        lines = pl.ds(pl.multiple_of(k * width, width), width)
        pre[0] += dot_tn(b2[k, fab.row], w_out[lines, :])
        return carry

    lax.fori_loop(0, count_k, last, 0)
    out[...] = pre[0].astype(BF)

    def product_in(k):
        left = b1[k].reshape(rows * pixels, width)
        return dot_tn(left, g1[...].reshape(rows * pixels, width))

    def weight_grad(product, result, sems, d):
        def store(slot):
            k = fab.z_at(d) * 2 + slot
            return pltpu.make_async_copy(
                stage.at[slot],
                result.at[pl.ds(pl.multiple_of(k * width, width), width), :],
                sems.at[slot],
            )

        def step(slot, carry):
            full = product(fab.z_at(d) * 2 + slot).astype(BF)
            if d > 0:
                store(slot).wait()
            stage[slot] = full
            store(slot).start()
            return carry

        lax.fori_loop(0, 2, step, 0)
        if d == fab.zs - 1:
            for slot in range(2):
                store(slot).wait()

    for d in depths:
        weight_grad(product_in, gw_in, local.at[pl.ds(2, 2)], d)
        gather2.pump_xy(d)

    def turn(q, carry):
        at = pl.ds(pl.multiple_of(q * pixels, pixels), pixels)
        act_t[:, at] = act[q].astype(F32).T.astype(BF)
        return carry

    lax.fori_loop(0, rows + 2, turn, 0)

    for b in range(3):

        def move(q, carry):
            value = gt[q + 1].astype(F32)
            value = moved(value, -1) if b == 0 else moved(value, 1) if b == 2 else value
            shifted[q] = value.astype(BF)
            return carry

        lax.fori_loop(0, rows, move, 0)

        def tap_grad(a, carry):
            for part in chunks:
                span = pl.ds(pl.multiple_of(a * pixels, pixels), rows * pixels)
                full = dot(act_t[part, span], shifted[:, :, part].reshape(rows * pixels, chunk))
                full = jnp.where(same, full, 0.0).reshape(chunk // gw, gw, chunk)
                gw_group[a * 3 + b, :, part] = jnp.sum(full, axis=0).astype(BF)
            return carry

        lax.fori_loop(0, 3, tap_grad, 0)

    for r in other_rows:
        fab.arrived(cots.at[r], cot_recv.at[r])
    stores = [pltpu.make_async_copy(cots, cot_rows, local.at[4])]
    stores[0].start()
    for d in depths:
        gather2.pump_d(d)
        for r in other_rows:
            gather2.from_twin(d, r)
        pair = pl.ds(fab.z_at(d) * 2, 2)
        stores.append(pltpu.make_async_copy(b2.at[pair], mids.at[pair], local.at[5 + d]))
        stores[-1].start()
    g_in[...] = (cot[...].astype(F32) + scatter2.finish()).astype(BF)
    for store in stores:
        store.wait()
    for copy in fab.sent:
        copy.wait_send()
    for go, copy in fab.held:

        @pl.when(go)
        def _():
            copy().wait_send()


def finish_kernel(*refs):
    out, g_in, gw_in, gw_group, mids, cots = refs[:6]
    results, gw_out = refs[6:10], refs[10]
    held = refs[11:15]
    mid, cot, product = refs[15:18]
    load_sems, store_sems, mid_sems, product_sems = refs[18:]
    count, rows, width, pixels = mids.shape
    load_cot = pltpu.make_async_copy(cots, cot, mid_sems.at[count])
    load_cot.start()

    def load_mid(k):
        return pltpu.make_async_copy(mids.at[k], mid.at[k], mid_sems.at[k])

    def store(k):
        lines = pl.ds(pl.multiple_of(k * width, width), width)
        return pltpu.make_async_copy(product.at[k], gw_out.at[lines, :], product_sems.at[k])

    for k in range(count):
        load_mid(k).start()
    copies = []
    for n, (src, via, dst) in enumerate(zip((out, g_in, gw_group, gw_in), held, results)):
        parts = 4 if n == 3 else 1
        size = src.shape[0] // parts
        for p in range(parts):
            at = pl.ds(p * size, size)
            load = pltpu.make_async_copy(src.at[at], via.at[at], load_sems.at[n, p])
            copies.append((load, pltpu.make_async_copy(via.at[at], dst.at[at], store_sems.at[n, p])))
            load.start()
    load_cot.wait()
    steps = 4
    each = count // steps

    def step(k, carry):
        load_mid(k).wait()
        left = jnp.concatenate([mid[k, r] for r in range(rows)], axis=1)
        product[k] = dot(left, cot[...].reshape(rows * pixels, width)).astype(BF)
        store(k).start()
        return carry

    for at in range(steps):
        lax.fori_loop(at * each, (at + 1) * each, step, 0)
        for load, onward in copies[2 * at : 2 * at + 2]:
            load.wait()
            onward.start()
    for load, onward in copies:
        onward.wait()
    for k in range(count):
        store(k).wait()


def body(features, w_in, w_group, w_out, cotangent):
    row_count, pixels, width = features.shape
    rows, lanes = lax.axis_size("row"), lax.axis_size("ch")
    total = rows * lanes * features.size * features.dtype.itemsize
    fits = (rows, lanes, row_count) == (4, 8, 1) and w_in.shape[1] == width == 512
    if not fits or total > GATHER_BYTES:
        return wide_body(features, w_in, w_group, w_out, cotangent)
    zs = lanes // 2
    channels = w_in.shape[0]
    gw = w_group.shape[2]
    dma = pltpu.SemaphoreType.DMA
    vmem = pltpu.VMEM
    gather_sems = [dma((lanes, rows)), dma((zs + 1,)), dma((6,)), dma((6,)), dma((rows * zs,))]
    part = vmem((zs, pixels, width), BF)
    scatter = [part, part, part, part, vmem((pixels, width), F32)]
    scatter += [dma((zs,)), dma((zs,)), dma((zs - 1,)), dma((zs,))]
    scratch = [
        vmem((lanes, rows, pixels, width), BF),
        vmem((lanes, rows, width, pixels), BF),
        vmem((channels, width), BF),
        vmem((channels, width), BF),
        vmem((rows, pixels, width), F32),
        vmem((rows + 2, pixels, width), BF),
        vmem((rows + 2, pixels, width), BF),
        vmem((rows, pixels, width), BF),
        vmem((rows, pixels, width), BF),
        vmem((rows, pixels, width), BF),
        vmem((9, width // 256, 256, 256), BF),
        vmem((2, width, width), BF),
    ]
    scratch += gather_sems * 2 + scatter * 2
    scratch += [dma((3,)), dma((rows,)), dma((3,)), dma((rows,)), dma((2,)), dma((2,)), dma((9,))]
    scratch += [vmem((width, (rows + 2) * pixels), BF)]
    in_vmem = pl.BlockSpec(memory_space=pltpu.VMEM)
    in_any = pl.BlockSpec(memory_space=pl.ANY)
    flat = jax.ShapeDtypeStruct((pixels, width), BF)
    weight = jax.ShapeDtypeStruct((channels, width), BF)
    taps = jax.ShapeDtypeStruct((9, gw, width), BF)
    mids = jax.ShapeDtypeStruct((lanes, rows, width, pixels), BF)
    cot_rows = jax.ShapeDtypeStruct((rows, pixels, width), BF)
    params = pltpu.CompilerParams(
        collective_id=0, has_side_effects=True, vmem_limit_bytes=60 * 1024 * 1024
    )
    out, g_in, gw_in, gw_group, mid_all, cot_all = pl.pallas_call(
        block_kernel,
        out_shape=[flat, flat, weight, taps, mids, cot_rows],
        in_specs=[in_vmem, in_any, in_vmem, in_any, in_vmem],
        out_specs=[in_vmem, in_vmem, in_any, in_vmem, in_any, in_any],
        scratch_shapes=scratch,
        compiler_params=params,
    )(
        features.reshape(pixels, width),
        w_in,
        w_group.reshape(9, gw, width),
        w_out,
        cotangent.reshape(pixels, width),
    )
    out, g_in, gw_group, gw_in, gw_out = pl.pallas_call(
        finish_kernel,
        out_shape=[flat, flat, taps, weight, weight],
        in_specs=[in_any] * 6,
        out_specs=[in_any] * 5,
        scratch_shapes=[vmem(v.shape, BF) for v in (flat, flat, taps, weight, mids, cot_rows)]
        + [vmem((lanes, width, width), BF)]
        + [dma((4, 4)), dma((4, 4)), dma((lanes + 1,)), dma((lanes,))],
        compiler_params=pltpu.CompilerParams(vmem_limit_bytes=60 * 1024 * 1024),
    )(out, g_in, gw_in, gw_group, mid_all, cot_all)
    return (
        out.reshape(features.shape),
        g_in.reshape(features.shape),
        gw_in,
        gw_group.reshape(w_group.shape),
        gw_out,
    )


def solution(mesh):
    placed = (
        P("row", None, "ch"),
        P(None, "ch"),
        P(None, None, None, "ch"),
        P(None, "ch"),
        P("row", None, "ch"),
    )
    return jax.shard_map(
        body,
        mesh=mesh,
        in_specs=placed,
        out_specs=(
            P("row", None, "ch"),
            P("row", None, "ch"),
            P(None, "ch"),
            P(None, None, None, "ch"),
            P(None, "ch"),
        ),
        check_vma=False,
    )
```

```python
import jax
import jax.numpy as jnp
from jax import lax
from jax.experimental import pallas as pl
from jax.experimental.pallas import tpu as pltpu
from jax.sharding import PartitionSpec as P


GATHER_BYTES = 8 * 1024 * 1024
MESH = pl.DeviceIdType.MESH
BF = jnp.bfloat16
F32 = jnp.float32


def padded_2(cells, sides, width):
    for axis, dim in sides:
        count = lax.axis_size(axis)
        ends = count - 1
        head = lax.slice_in_dim(cells, 0, width, axis=dim)
        tail = lax.slice_in_dim(cells, cells.shape[dim] - width, cells.shape[dim], axis=dim)
        cells = jnp.concatenate(
            [
                lax.ppermute(tail, axis, [(i, (i + 1) % count) for i in range(ends)]),
                cells,
                lax.ppermute(head, axis, [((i + 1) % count, i) for i in range(ends)]),
            ],
            axis=dim,
        )
    return cells


def silu_slope(values):
    sigma = jax.nn.sigmoid(values)
    return sigma * (1.0 + values * (1.0 - sigma))


def full_channels(local):
    return lax.all_gather(local, "ch", axis=2, tiled=True)


def row_rims(local):
    padded = padded_2(local, (("row", 0),), 1)
    return jnp.pad(padded, ((0, 0), (1, 1), (0, 0)))


def group_view(local, group_width):
    return local.reshape(local.shape[0], local.shape[1], local.shape[2] // group_width, group_width)


def wide_body(features, w_in, w_group, w_out, cotangent):
    row_count, col_count, local_ch = features.shape
    group_width = w_group.shape[2]
    local_mid = w_in.shape[1]
    pixel_count = row_count * col_count
    gathered = full_channels(features)
    flat_in = gathered.reshape(pixel_count, -1)
    pre_one = jnp.dot(flat_in, w_in, preferred_element_type=jnp.float32)
    act_one = jax.nn.silu(pre_one).astype(jnp.bfloat16).reshape(row_count, col_count, local_mid)
    padded_one = group_view(row_rims(act_one), group_width)
    filters = w_group.reshape(3, 3, group_width, local_mid // group_width, group_width)
    pre_two = jnp.zeros((row_count, col_count, local_mid // group_width, group_width), jnp.float32)
    for row_tap in range(3):
        for col_tap in range(3):
            window = padded_one[row_tap : row_tap + row_count, col_tap : col_tap + col_count]
            pre_two = pre_two + jnp.einsum(
                "rcgi,igj->rcgj",
                window,
                filters[row_tap, col_tap],
                preferred_element_type=jnp.float32,
            )
    pre_two = pre_two.reshape(pixel_count, local_mid)
    act_two = jax.nn.silu(pre_two).astype(jnp.bfloat16)
    mid_full = full_channels(act_two.reshape(row_count, col_count, local_mid)).reshape(
        pixel_count, -1
    )
    branch = jnp.dot(mid_full, w_out, preferred_element_type=jnp.float32)
    flat_local = features.reshape(pixel_count, local_ch)
    block_out = (
        (flat_local.astype(jnp.float32) + branch)
        .astype(jnp.bfloat16)
        .reshape(row_count, col_count, local_ch)
    )
    grad_flat = cotangent.reshape(pixel_count, local_ch)
    partial = lax.dot_general(
        w_out, grad_flat, (((1,), (1,)), ((), ())), preferred_element_type=jnp.float32
    ).astype(jnp.bfloat16)
    d_two = (
        lax.psum_scatter(partial, "ch", scatter_dimension=0, tiled=True).astype(jnp.float32).T
    )
    grad_two = (d_two * silu_slope(pre_two)).astype(jnp.bfloat16)
    padded_two = group_view(
        row_rims(grad_two.reshape(row_count, col_count, local_mid)), group_width
    )
    d_one = jnp.zeros((row_count, col_count, local_mid // group_width, group_width), jnp.float32)
    for row_tap in range(3):
        for col_tap in range(3):
            window = padded_two[
                2 - row_tap : 2 - row_tap + row_count, 2 - col_tap : 2 - col_tap + col_count
            ]
            d_one = d_one + jnp.einsum(
                "rcgj,igj->rcgi",
                window,
                filters[row_tap, col_tap],
                preferred_element_type=jnp.float32,
            )
    grad_one = (d_one.reshape(pixel_count, local_mid) * silu_slope(pre_one)).astype(jnp.bfloat16)
    grad_view = group_view(grad_two.reshape(row_count, col_count, local_mid), group_width)
    tap_rows = []
    for row_tap in range(3):
        tap_line = []
        for col_tap in range(3):
            window = padded_one[row_tap : row_tap + row_count, col_tap : col_tap + col_count]
            tap_line.append(
                jnp.einsum("rcgi,rcgj->igj", window, grad_view, preferred_element_type=jnp.float32)
            )
        tap_rows.append(jnp.stack(tap_line))
    group_grad = jnp.stack(tap_rows).reshape(3, 3, group_width, local_mid)
    rows = lax.axis_size("row")
    spread = rows * flat_in.size * flat_in.dtype.itemsize <= GATHER_BYTES
    left_in, right_in, left_out, right_out = flat_in, grad_one, mid_full, grad_flat
    if spread:
        left_in, right_in, left_out, right_out = (
            lax.all_gather(v, "row", axis=0, tiled=True)
            for v in (flat_in, grad_one, mid_full, grad_flat)
        )
    in_grad = lax.dot_general(
        left_in, right_in, (((0,), (0,)), ((), ())), preferred_element_type=jnp.float32
    ).astype(jnp.bfloat16)
    out_grad = lax.dot_general(
        left_out, right_out, (((0,), (0,)), ((), ())), preferred_element_type=jnp.float32
    ).astype(jnp.bfloat16)
    if not spread:
        in_grad, out_grad = lax.psum((in_grad, out_grad), "row")
    d_input = (
        lax.psum_scatter(
            lax.dot_general(
                w_in, grad_one, (((1,), (1,)), ((), ())), preferred_element_type=jnp.float32
            ).astype(jnp.bfloat16),
            "ch",
            scatter_dimension=0,
            tiled=True,
        )
        .astype(jnp.float32)
        .T
    )
    grad_input = (
        (grad_flat.astype(jnp.float32) + d_input)
        .astype(jnp.bfloat16)
        .reshape(row_count, col_count, local_ch)
    )
    group_grad = lax.psum(group_grad.astype(jnp.bfloat16), "row")
    return block_out, grad_input, in_grad, group_grad, out_grad


def dot(a, b):
    return jnp.dot(a, b, preferred_element_type=F32)


def dot_nt(a, b):
    return lax.dot_general(a, b, (((1,), (1,)), ((), ())), preferred_element_type=F32)


def dot_tn(a, b):
    return lax.dot_general(a, b, (((0,), (0,)), ((), ())), preferred_element_type=F32)


def moved(values, step):
    count = values.shape[0]
    at = lax.broadcasted_iota(jnp.int32, values.shape, 0)
    edge = 0 if step == 1 else count - 1
    return jnp.where(at == edge, 0.0, pltpu.roll(values, step % count, 0))


class Fabric:
    def __init__(self):
        self.row = lax.axis_index("row")
        self.ch = lax.axis_index("ch")
        self.core = lax.rem(self.ch, 2)
        self.z = self.ch // 2
        self.zs = lax.axis_size("ch") // 2
        x, y = lax.rem(self.row, 2), self.row // 2
        self.row_x = y * 2 + (1 - x)
        self.row_y = (1 - y) * 2 + x
        self.row_d = (1 - y) * 2 + (1 - x)
        self.twin = self.z * 2 + (1 - self.core)
        self.sent = []
        self.held = []

    def z_at(self, d):
        return lax.rem(self.z + d, self.zs)

    def ch_at(self, d):
        return self.z_at(d) * 2 + self.core

    def partners(self):
        out = [(self.row, self.ch_at(d)) for d in range(1, self.zs)]
        out += [(r, self.ch) for r in (self.row_x, self.row_y, self.row_d)]
        return out + [(self.row, self.twin)]

    def send(self, src, dst, send_sem, recv_sem, device):
        copy = pltpu.make_async_remote_copy(
            src_ref=src,
            dst_ref=dst,
            send_sem=send_sem,
            recv_sem=recv_sem,
            device_id=device,
            device_id_type=MESH,
        )
        copy.start()
        self.sent.append(copy)

    def arrived(self, dst, sem):
        pltpu.make_async_remote_copy(
            src_ref=dst,
            dst_ref=dst,
            send_sem=sem,
            recv_sem=sem,
            device_id=(self.row, self.twin),
            device_id_type=MESH,
        ).wait_recv()


class Gather:
    def __init__(self, fab, buf, recv, send_z, send_x, send_y, send_t):
        self.fab, self.buf, self.recv = fab, buf, recv
        self.send_z, self.send_x, self.send_y, self.send_t = send_z, send_x, send_y, send_t

    def push(self, k, r, send_sem, device):
        slot = self.buf.at[k, r]
        self.fab.send(slot, slot, send_sem, self.recv.at[k, r], device)

    def to_x(self, k, r, n):
        self.push(k, r, self.send_x.at[n], (self.fab.row_x, self.fab.ch))

    def to_y(self, k, r, n):
        self.push(k, r, self.send_y.at[n], (self.fab.row_y, self.fab.ch))

    def to_twin(self, k, r, n):
        self.push(k, r, self.send_t.at[n], (self.fab.row, self.fab.twin))

    def wait(self, k, r):
        self.fab.arrived(self.buf.at[k, r], self.recv.at[k, r])

    def start(self):
        f = self.fab
        self.relay(0, 1)
        self.relay(0, -1)
        self.to_x(f.ch, f.row, 0)
        self.to_y(f.ch, f.row, 0)
        self.to_twin(f.ch, f.row, 0)

    def relay(self, d, way):
        f = self.fab
        k = f.ch_at(d)
        slot = self.buf.at[k, f.row]
        sem = self.send_z.at[f.zs if d == 0 and way == 1 else d]

        def copy():
            return pltpu.make_async_remote_copy(
                src_ref=slot,
                dst_ref=slot,
                send_sem=sem,
                recv_sem=self.recv.at[k, f.row],
                device_id=(f.row, f.ch + 2 * way),
                device_id_type=MESH,
            )

        above = f.z + d < f.zs
        came = True if d == 0 else above if way == -1 else jnp.logical_not(above)
        more = f.z > 0 if way == -1 else f.z < f.zs - 1
        go = more if d == 0 else jnp.logical_and(came, more)

        @pl.when(go)
        def _():
            copy().start()

        f.held.append((go, copy))

    def land_z(self, step):
        f = self.fab
        for d, way in ((step, -1), (f.zs - step, 1)):
            here = f.z + d < f.zs if way == -1 else f.z + d >= f.zs

            @pl.when(here)
            def _():
                self.wait(f.ch_at(d), f.row)

            self.relay(d, way)

            @pl.when(here)
            def _():
                self.twin_copy(d).start()

    def twin_copy(self, d):
        f = self.fab
        slot = self.buf.at[f.ch_at(d), f.row]
        return pltpu.make_async_remote_copy(
            src_ref=slot,
            dst_ref=slot,
            send_sem=self.send_t.at[d],
            recv_sem=self.recv.at[f.ch_at(d), f.row],
            device_id=(f.row, f.twin),
            device_id_type=MESH,
        )

    def landed_z(self):
        for d in range(1, self.fab.zs):
            self.fab.sent.append(self.twin_copy(d))

    def spread_z(self, d):
        f = self.fab
        self.to_x(f.ch_at(d), f.row, d)
        self.to_y(f.ch_at(d), f.row, d)

    def pump_xy(self, d):
        f = self.fab
        half = f.zs // 2
        k = f.ch_at(d)
        self.wait(k, f.row_x)
        if d < half:
            self.to_y(k, f.row_x, f.zs + d)
        self.to_twin(k, f.row_x, f.zs + d)
        self.wait(k, f.row_y)
        if d >= half:
            self.to_x(k, f.row_y, f.zs + d - half)
        self.to_twin(k, f.row_y, 2 * f.zs + d)

    def pump_d(self, d):
        f = self.fab
        k = f.ch_at(d)
        self.wait(k, f.row_d)
        self.to_twin(k, f.row_d, 3 * f.zs + d)

    def from_twin(self, d, r):
        f = self.fab
        self.wait(f.z_at(d) * 2 + (1 - f.core), r)


class Scatter:
    def __init__(self, fab, give, got, out, far, acc, give_s, got_s, out_s, far_s):
        self.fab, self.give, self.got, self.out, self.far, self.acc = fab, give, got, out, far, acc
        self.give_s, self.got_s, self.out_s, self.far_s = give_s, got_s, out_s, far_s

    def part(self, lhs, w_ref, k):
        width = lhs.shape[1]
        rows = pl.ds(pl.multiple_of(k * width, width), width)
        return dot_nt(lhs, w_ref[rows, :])

    def start(self, lhs, w_ref):
        f = self.fab
        for d in (1, 2, 3, 0):
            at = f.z_at(d)
            self.give[at] = self.part(lhs, w_ref, at * 2 + (1 - f.core)).astype(BF)
            f.send(
                self.give.at[at],
                self.got.at[at],
                self.give_s.at[d],
                self.got_s.at[at],
                (f.row, f.twin),
            )

    def middle(self, lhs, w_ref):
        f = self.fab
        for d in (1, 2, 3, 0):
            at = f.z_at(d)
            own = self.part(lhs, w_ref, at * 2 + f.core)
            f.arrived(self.got.at[at], self.got_s.at[at])
            own = own + self.got[at].astype(F32)
            if d == 0:
                self.acc[...] = own
            else:
                self.out[at] = own.astype(BF)
                f.send(
                    self.out.at[at],
                    self.far.at[f.z],
                    self.out_s.at[d - 1],
                    self.far_s.at[f.z],
                    (f.row, f.ch_at(d)),
                )

    def finish(self):
        f = self.fab
        for d in (1, 2, 3):
            at = f.z_at(d)
            f.arrived(self.far.at[at], self.far_s.at[at])
        total = self.acc[...]
        for d in (1, 2, 3):
            total = total + self.far[f.z_at(d)].astype(F32)
        return total


def block_kernel(*refs):
    (feat, w_in_hbm, wg, w_out_hbm, cot, out, g_in, gw_in, gw_group, mids, cot_rows) = refs[:11]
    refs = refs[1:]
    (b1, b2, w_in, w_out, pre, act, gt, g1, cots, shifted, wide, stage) = refs[10:22]
    act_t = refs[57]
    (r1, z1, x1, y1, t1, r2, z2, x2, y2, t2) = refs[22:32]
    s1, s2 = refs[32:41], refs[41:50]
    cot_send, cot_recv, gt_send, gt_recv, halo_send, halo_recv, local = refs[50:57]
    fab = Fabric()
    rows = cots.shape[0]
    pixels, width = feat.shape
    chunk = wide.shape[2]
    gw = wg.shape[1]
    count_k = b1.shape[0]
    chunks = [slice(i * chunk, (i + 1) * chunk) for i in range(width // chunk)]

    load_out = pltpu.make_async_copy(w_out_hbm, w_out, local.at[0])
    load_in = pltpu.make_async_copy(w_in_hbm, w_in, local.at[1])
    load_out.start()
    load_in.start()
    barrier = pltpu.get_barrier_semaphore()
    partners = fab.partners()
    for device in partners:
        pl.semaphore_signal(barrier, inc=1, device_id=device, device_id_type=MESH)
    pl.semaphore_wait(barrier, len(partners))

    gather1 = Gather(fab, b1, r1, z1, x1, y1, t1)
    gather2 = Gather(fab, b2, r2, z2, x2, y2, t2)
    scatter1 = Scatter(fab, *s1)
    scatter2 = Scatter(fab, *s2)
    other_rows = (fab.row_x, fab.row_y, fab.row_d)

    b1[fab.ch, fab.row] = feat[...]
    gather1.start()
    cots[fab.row] = cot[...]
    for n, r in enumerate(other_rows):
        fab.send(
            cots.at[fab.row],
            cots.at[fab.row],
            cot_send.at[n],
            cot_recv.at[fab.row],
            (r, fab.ch),
        )
    load_out.wait()
    scatter1.start(cot[...], w_out)

    blank = jnp.zeros((pixels, width), BF)
    act[0] = blank
    act[rows + 1] = blank
    gt[0] = blank
    gt[rows + 1] = blank
    row_group = lax.broadcasted_iota(jnp.int32, (chunk, chunk), 0) // gw
    col_group = lax.broadcasted_iota(jnp.int32, (chunk, chunk), 1) // gw
    same = row_group == col_group

    def widen(tap, carry):
        for i, part in enumerate(chunks):
            taps = wg[tap, :, part].astype(F32)
            dense = jnp.concatenate([taps] * (chunk // gw), axis=0)
            wide[tap, i] = jnp.where(same, dense, 0.0).astype(BF)
        return carry

    lax.fori_loop(0, 9, widen, 0)

    depths = range(fab.zs)
    load_in.wait()

    def activate(r):
        value = pre[r]
        act[r + 1] = (value * jax.nn.sigmoid(value)).astype(BF)

    def first_xy(d):
        for r in (fab.row_x, fab.row_y):
            gather1.from_twin(d, r)

        def add(i, carry):
            r = fab.row_x + lax.rem(i, 2) * (fab.row_y - fab.row_x)
            k = fab.z_at(d) * 2 + i // 2
            lines = pl.ds(pl.multiple_of(k * width, width), width)
            pre[r] += dot(b1[k, r], w_in[lines, :])
            return carry

        lax.fori_loop(0, 4, add, 0)

    def first(r):
        for d in depths:
            gather1.from_twin(d, r)
        pre[r] = jnp.zeros((pixels, width), F32)

        def add(k, carry):
            lines = pl.ds(pl.multiple_of(k * width, width), width)
            pre[r] += dot(b1[k, r], w_in[lines, :])
            return carry

        lax.fori_loop(0, count_k, add, 0)
        activate(r)

    for d in depths[1:]:
        gather1.land_z(d)
    gather1.landed_z()
    first(fab.row)
    above, below = fab.row > 0, fab.row < rows - 1

    def halo(n, r):
        return pltpu.make_async_remote_copy(
            src_ref=act.at[fab.row + 1],
            dst_ref=act.at[fab.row + 1],
            send_sem=halo_send.at[n],
            recv_sem=halo_recv.at[n],
            device_id=(r, fab.ch),
            device_id_type=MESH,
        )

    def halo_from(n, r):
        return pltpu.make_async_remote_copy(
            src_ref=act.at[r + 1],
            dst_ref=act.at[r + 1],
            send_sem=halo_send.at[n],
            recv_sem=halo_recv.at[n],
            device_id=(r, fab.ch),
            device_id_type=MESH,
        )

    @pl.when(above)
    def _():
        halo(0, fab.row - 1).start()

    @pl.when(below)
    def _():
        halo(1, fab.row + 1).start()

    for d in depths[1:]:
        gather1.spread_z(d)
    scatter1.middle(cot[...], w_out)

    @pl.when(above)
    def _():
        halo(0, fab.row - 1).wait_send()
        halo_from(1, fab.row - 1).wait_recv()

    @pl.when(below)
    def _():
        halo(1, fab.row + 1).wait_send()
        halo_from(0, fab.row + 1).wait_recv()

    taps_of = [[a * 3 + b for a in range(3)] for b in range(3)]
    two = []
    for i, part in enumerate(chunks):
        total = None
        for b in range(3):
            side = None
            for a in range(3):
                term = dot(act[fab.row + a, :, part], wide[taps_of[b][a], i])
                side = term if side is None else side + term
            side = moved(side, 1) if b == 0 else moved(side, -1) if b == 2 else side
            total = side if total is None else total + side
        two.append(total)
    slopes = []
    for i, part in enumerate(chunks):
        b2[fab.ch, fab.row, part, :] = (two[i] * jax.nn.sigmoid(two[i])).T.astype(BF)
        slopes.append(silu_slope(two[i]))
    gather2.start()
    pre[fab.row_x] = jnp.zeros((pixels, width), F32)
    pre[fab.row_y] = jnp.zeros((pixels, width), F32)
    gather1.pump_xy(0)
    gather1.pump_xy(1)
    first_xy(0)
    gather2.land_z(1)
    gather1.pump_xy(2)
    first_xy(1)
    gather2.land_z(2)
    gather1.pump_xy(3)
    first_xy(2)
    d_two = scatter1.finish()
    for i, part in enumerate(chunks):
        gt[fab.row + 1, :, part] = (d_two[:, part] * slopes[i]).astype(BF)
    for n, r in enumerate(other_rows):
        fab.send(
            gt.at[fab.row + 1],
            gt.at[fab.row + 1],
            gt_send.at[n],
            gt_recv.at[fab.row],
            (r, fab.ch),
        )
    first_xy(3)
    gather2.land_z(3)
    gather2.landed_z()
    for d in depths[1:]:
        gather2.spread_z(d)
    for d in depths:
        gather1.pump_d(d)
    gather2.pump_xy(0)
    activate(fab.row_x)
    activate(fab.row_y)
    first(fab.row_d)
    for r in other_rows:
        fab.arrived(gt.at[r + 1], gt_recv.at[r])

    def back(q, carry):
        for i, part in enumerate(chunks):
            total = None
            for b in range(3):
                side = None
                for a in range(3):
                    term = dot_nt(gt[q + 2 - a, :, part], wide[taps_of[b][a], i])
                    side = term if side is None else side + term
                side = moved(side, -1) if b == 0 else moved(side, 1) if b == 2 else side
                total = side if total is None else total + side
            g1[q, :, part] = (total * silu_slope(pre[q, :, part])).astype(BF)
        return carry

    lax.fori_loop(0, rows, back, 0)
    scatter2.start(g1[fab.row], w_in)
    scatter2.middle(g1[fab.row], w_in)
    gather2.pump_xy(1)

    def product_in(k):
        left = b1[k].reshape(rows * pixels, width)
        return dot_tn(left, g1[...].reshape(rows * pixels, width))

    def weight_grad(product, result, sems, d):
        def store(slot):
            k = fab.z_at(d) * 2 + slot
            return pltpu.make_async_copy(
                stage.at[slot],
                result.at[pl.ds(pl.multiple_of(k * width, width), width), :],
                sems.at[slot],
            )

        def step(slot, carry):
            full = product(fab.z_at(d) * 2 + slot).astype(BF)
            if d > 0:
                store(slot).wait()
            stage[slot] = full
            store(slot).start()
            return carry

        lax.fori_loop(0, 2, step, 0)
        if d == fab.zs - 1:
            for slot in range(2):
                store(slot).wait()

    for d in depths:
        weight_grad(product_in, gw_in, local.at[pl.ds(2, 2)], d)
        if d + 2 < fab.zs:
            gather2.pump_xy(d + 2)

    for d in depths:
        gather2.from_twin(d, fab.row)
    pre[0] = feat[...].astype(F32)

    def last(k, carry):
        lines = pl.ds(pl.multiple_of(k * width, width), width)
        pre[0] += dot_tn(b2[k, fab.row], w_out[lines, :])
        return carry

    lax.fori_loop(0, count_k, last, 0)
    out[...] = pre[0].astype(BF)

    def turn(q, carry):
        at = pl.ds(pl.multiple_of(q * pixels, pixels), pixels)
        act_t[:, at] = act[q].astype(F32).T.astype(BF)
        return carry

    lax.fori_loop(0, rows + 2, turn, 0)

    for b in range(3):

        def move(q, carry):
            value = gt[q + 1].astype(F32)
            value = moved(value, -1) if b == 0 else moved(value, 1) if b == 2 else value
            shifted[q] = value.astype(BF)
            return carry

        lax.fori_loop(0, rows, move, 0)

        def tap_grad(a, carry):
            for part in chunks:
                span = pl.ds(pl.multiple_of(a * pixels, pixels), rows * pixels)
                full = dot(act_t[part, span], shifted[:, :, part].reshape(rows * pixels, chunk))
                full = jnp.where(same, full, 0.0).reshape(chunk // gw, gw, chunk)
                gw_group[a * 3 + b, :, part] = jnp.sum(full, axis=0).astype(BF)
            return carry

        lax.fori_loop(0, 3, tap_grad, 0)

    for r in other_rows:
        fab.arrived(cots.at[r], cot_recv.at[r])
    stores = [pltpu.make_async_copy(cots, cot_rows, local.at[4])]
    stores[0].start()
    for d in depths:
        gather2.pump_d(d)
        for r in other_rows:
            gather2.from_twin(d, r)
        pair = pl.ds(fab.z_at(d) * 2, 2)
        stores.append(pltpu.make_async_copy(b2.at[pair], mids.at[pair], local.at[5 + d]))
        stores[-1].start()
    g_in[...] = (cot[...].astype(F32) + scatter2.finish()).astype(BF)
    for store in stores:
        store.wait()
    for copy in fab.sent:
        copy.wait_send()
    for go, copy in fab.held:

        @pl.when(go)
        def _():
            copy().wait_send()


def finish_kernel(*refs):
    out, g_in, gw_in, gw_group, mids, cots = refs[:6]
    results, gw_out = refs[6:10], refs[10]
    held = refs[11:15]
    mid, cot, product = refs[15:18]
    load_sems, store_sems, mid_sems, product_sems = refs[18:]
    count, rows, width, pixels = mids.shape
    load_cot = pltpu.make_async_copy(cots, cot, mid_sems.at[count])
    load_cot.start()

    def load_mid(k):
        return pltpu.make_async_copy(mids.at[k], mid.at[k], mid_sems.at[k])

    def store(k):
        lines = pl.ds(pl.multiple_of(k * width, width), width)
        return pltpu.make_async_copy(product.at[k], gw_out.at[lines, :], product_sems.at[k])

    for k in range(count):
        load_mid(k).start()
    copies = []
    for n, (src, via, dst) in enumerate(zip((out, g_in, gw_group, gw_in), held, results)):
        parts = 4 if n == 3 else 1
        size = src.shape[0] // parts
        for p in range(parts):
            at = pl.ds(p * size, size)
            load = pltpu.make_async_copy(src.at[at], via.at[at], load_sems.at[n, p])
            copies.append((load, pltpu.make_async_copy(via.at[at], dst.at[at], store_sems.at[n, p])))
            load.start()
    load_cot.wait()
    steps = 4
    each = count // steps

    def step(k, carry):
        load_mid(k).wait()
        left = jnp.concatenate([mid[k, r] for r in range(rows)], axis=1)
        product[k] = dot(left, cot[...].reshape(rows * pixels, width)).astype(BF)
        store(k).start()
        return carry

    for at in range(steps):
        lax.fori_loop(at * each, (at + 1) * each, step, 0)
        for load, onward in copies[2 * at : 2 * at + 2]:
            load.wait()
            onward.start()
    for load, onward in copies:
        onward.wait()
    for k in range(count):
        store(k).wait()


def body(features, w_in, w_group, w_out, cotangent):
    row_count, pixels, width = features.shape
    rows, lanes = lax.axis_size("row"), lax.axis_size("ch")
    total = rows * lanes * features.size * features.dtype.itemsize
    fits = (rows, lanes, row_count) == (4, 8, 1) and w_in.shape[1] == width == 512
    if not fits or total > GATHER_BYTES:
        return wide_body(features, w_in, w_group, w_out, cotangent)
    zs = lanes // 2
    channels = w_in.shape[0]
    gw = w_group.shape[2]
    dma = pltpu.SemaphoreType.DMA
    vmem = pltpu.VMEM
    gather_sems = [dma((lanes, rows)), dma((zs + 1,)), dma((6,)), dma((6,)), dma((rows * zs,))]
    part = vmem((zs, pixels, width), BF)
    scatter = [part, part, part, part, vmem((pixels, width), F32)]
    scatter += [dma((zs,)), dma((zs,)), dma((zs - 1,)), dma((zs,))]
    scratch = [
        vmem((lanes, rows, pixels, width), BF),
        vmem((lanes, rows, width, pixels), BF),
        vmem((channels, width), BF),
        vmem((channels, width), BF),
        vmem((rows, pixels, width), F32),
        vmem((rows + 2, pixels, width), BF),
        vmem((rows + 2, pixels, width), BF),
        vmem((rows, pixels, width), BF),
        vmem((rows, pixels, width), BF),
        vmem((rows, pixels, width), BF),
        vmem((9, width // 256, 256, 256), BF),
        vmem((2, width, width), BF),
    ]
    scratch += gather_sems * 2 + scatter * 2
    scratch += [dma((3,)), dma((rows,)), dma((3,)), dma((rows,)), dma((2,)), dma((2,)), dma((9,))]
    scratch += [vmem((width, (rows + 2) * pixels), BF)]
    in_vmem = pl.BlockSpec(memory_space=pltpu.VMEM)
    in_any = pl.BlockSpec(memory_space=pl.ANY)
    flat = jax.ShapeDtypeStruct((pixels, width), BF)
    weight = jax.ShapeDtypeStruct((channels, width), BF)
    taps = jax.ShapeDtypeStruct((9, gw, width), BF)
    mids = jax.ShapeDtypeStruct((lanes, rows, width, pixels), BF)
    cot_rows = jax.ShapeDtypeStruct((rows, pixels, width), BF)
    params = pltpu.CompilerParams(
        collective_id=0, has_side_effects=True, vmem_limit_bytes=60 * 1024 * 1024
    )
    out, g_in, gw_in, gw_group, mid_all, cot_all = pl.pallas_call(
        block_kernel,
        out_shape=[flat, flat, weight, taps, mids, cot_rows],
        in_specs=[in_vmem, in_any, in_vmem, in_any, in_vmem],
        out_specs=[in_vmem, in_vmem, in_any, in_vmem, in_any, in_any],
        scratch_shapes=scratch,
        compiler_params=params,
    )(
        features.reshape(pixels, width),
        w_in,
        w_group.reshape(9, gw, width),
        w_out,
        cotangent.reshape(pixels, width),
    )
    out, g_in, gw_group, gw_in, gw_out = pl.pallas_call(
        finish_kernel,
        out_shape=[flat, flat, taps, weight, weight],
        in_specs=[in_any] * 6,
        out_specs=[in_any] * 5,
        scratch_shapes=[vmem(v.shape, BF) for v in (flat, flat, taps, weight, mids, cot_rows)]
        + [vmem((lanes, width, width), BF)]
        + [dma((4, 4)), dma((4, 4)), dma((lanes + 1,)), dma((lanes,))],
        compiler_params=pltpu.CompilerParams(vmem_limit_bytes=60 * 1024 * 1024),
    )(out, g_in, gw_in, gw_group, mid_all, cot_all)
    return (
        out.reshape(features.shape),
        g_in.reshape(features.shape),
        gw_in,
        gw_group.reshape(w_group.shape),
        gw_out,
    )


def solution(mesh):
    placed = (
        P("row", None, "ch"),
        P(None, "ch"),
        P(None, None, None, "ch"),
        P(None, "ch"),
        P("row", None, "ch"),
    )
    return jax.shard_map(
        body,
        mesh=mesh,
        in_specs=placed,
        out_specs=(
            P("row", None, "ch"),
            P("row", None, "ch"),
            P(None, "ch"),
            P(None, None, None, "ch"),
            P(None, "ch"),
        ),
        check_vma=False,
    )
```
